32 devices in a mesh: row: 8 (over z, y), col: 4 (over x, core).
Axes of the slice: x: 2, y: 2, z: 4, core: 2. Of those that a mesh axis runs over, the one named last changes fastest.
Arguments:
- positions: float32 [3, 4096], P(None, ('row', 'col')), may hold values from 0 to 1
- radii: float32 [4096], P(('row', 'col')), may hold values from 0.5 to 2
- right_side: float32 [4096, 256], P(('row', 'col')), may hold values from -60 to 60, as said below
Outputs:
- solution: float32 [4096, 256], P(('row', 'col'))
- residual: float32 [4096, 256], P(('row', 'col'))
The draws below stay inside these ranges and needn't reach their ends.
Inputs may be any that keep to these rules, and one draw needn't show every extreme that they name: `right_side`: real values of varying scale.
All inputs are finite; a program needn't handle non-finite values.
Results may differ from the reference program's by a relative error of at most 0.0003.
Values sent between devices are 32-bit elements; how exact they have to be, the bound alone decides.
No kernel may reach another device: no remote copies, remote signals or barrier semaphores. Data moves between devices by JAX's collectives and lax.ppermute only.
A program may use at most 64 MiB of HBM per device.

```python
import math
import jax
import jax.numpy as jnp
from jax import lax

NRHS = 256
ITERS = 2
NP = 4096


def draw_right_side(key, part):
    key_rows, key_cols, key_base = jax.random.split(key, 3)
    growth_ramp = jnp.exp(jnp.log(3.0) * jnp.arange(NP, dtype=jnp.float32) / NP)
    row_factor = jnp.exp(jax.random.uniform(key_rows, (NP, 1), minval=0.0, maxval=jnp.log(10.0)))
    col_factor = jnp.exp(jax.random.uniform(key_cols, (1, NRHS), minval=jnp.log(0.5), maxval=jnp.log(2.0)))
    base_draw = jnp.clip(jax.random.normal(key_base, (NP, NRHS)), -6.0, 6.0)
    scaled = base_draw * growth_ramp[:, None] * row_factor * col_factor / 6.0
    return scaled.astype(jnp.float32)


def block_levels(stream_key, extent, pieces, least, top_value):
    factor_of = 1.0
    for dim, shards_of in pieces:
        heights = jax.random.uniform(jax.random.fold_in(jax.random.fold_in(stream_key, 6), dim), (shards_of,), jnp.float32, least / len(pieces), top_value / len(pieces))
        factor_of = factor_of * jnp.repeat(jnp.exp(heights), extent[dim] // shards_of).reshape((-1,) + (1,) * (len(extent) - 1 - dim))
    return factor_of


def setup_inputs(seed: int = 0) -> dict:
    streams_of = jax.random.split(jax.random.key(seed), 4)
    return {
        "positions": jnp.clip(1.0 * jax.random.uniform(streams_of[0], (3, NP), jnp.float32) ** block_levels(streams_of[0], (3, NP), ((1, 32),), -0.2, 0.2), 0.0, 1.0),
        "radii": jnp.clip(jnp.exp(math.log(2.0) - 1.3862944 * jax.random.uniform(streams_of[1], (NP,), jnp.float32) ** block_levels(streams_of[1], (NP,), ((0, 32),), -0.2, 0.2)), 0.5, 2.0),
        "right_side": draw_right_side(jax.random.fold_in(streams_of[3], 71), 0),
    }


def kernel_product(row_points, col_points, values, kernel_scale, softening, limit):
    row_count = row_points.shape[1]
    col_count = col_points.shape[1]
    blocks = max(1, row_count * col_count // limit)
    while row_count % blocks:
        blocks = blocks - 1
    block_size = row_count // blocks
    grouped = row_points.reshape(3, blocks, block_size).transpose(1, 0, 2)

    def apply_block(row_block):
        first = row_block[0][:, None] - col_points[0][None, :]
        second = row_block[1][:, None] - col_points[1][None, :]
        third = row_block[2][:, None] - col_points[2][None, :]
        squared = first * first + second * second + third * third
        weights = lax.rsqrt(squared + softening) * kernel_scale
        return jnp.dot(weights, values, preferred_element_type=jnp.float32, precision=lax.Precision.HIGHEST)
    return lax.map(apply_block, grouped).reshape(row_count, values.shape[1])

def constants(total):
    kernel_scale = float(total) ** (-0.5)
    spacing = 0.25 * float(total) ** (-1.0 / 3.0)
    return (kernel_scale, spacing * spacing)

def reference(positions, radii, right_side):
    kernel_scale, softening = constants(NP)

    def operator(vector):
        coupled = kernel_product(positions, positions, vector, kernel_scale, softening, 1 << 22)
        return vector / radii[:, None] + coupled
    solution = jnp.zeros_like(right_side)
    residual = right_side
    direction = right_side
    norm_now = lax.optimization_barrier(jnp.sum(residual * residual, axis=0))
    for iteration in range(ITERS):
        image_vec = operator(direction)
        step_size = norm_now / lax.optimization_barrier(jnp.sum(direction * image_vec, axis=0))
        solution = solution + step_size * direction
        residual = residual - step_size * image_vec
        if iteration + 1 < ITERS:
            norm_next = lax.optimization_barrier(jnp.sum(residual * residual, axis=0))
            direction = residual + norm_next / norm_now * direction
            norm_now = norm_next
    return (solution, residual)
```

```python
import functools

import jax
import jax.numpy as jnp
from jax import lax
from jax.experimental import pallas as pl
from jax.experimental.pallas import tpu as pltpu
from jax.sharding import PartitionSpec as P

ITERS = 2
AXES = ("row", "col")
F32 = jnp.float32
BF16 = jnp.bfloat16
LANES = 128
EXTRA = 8
VM = pl.BlockSpec(memory_space=pltpu.VMEM)
KERNEL_BYTES = 32 << 20


def constants(total):
    kernel_scale = float(total) ** (-0.5)
    spacing = 0.25 * float(total) ** (-1.0 / 3.0)
    return (kernel_scale, spacing * spacing)


def kernel_product(row_points, col_points, values, kernel_scale, softening, limit):
    row_count = row_points.shape[1]
    col_count = col_points.shape[1]
    blocks = max(1, row_count * col_count // limit)
    while row_count % blocks:
        blocks = blocks - 1
    block_size = row_count // blocks
    grouped = row_points.reshape(3, blocks, block_size).transpose(1, 0, 2)

    def apply_block(row_block):
        first = row_block[0][:, None] - col_points[0][None, :]
        second = row_block[1][:, None] - col_points[1][None, :]
        third = row_block[2][:, None] - col_points[2][None, :]
        squared = first * first + second * second + third * third
        weights = lax.rsqrt(squared + softening) * kernel_scale
        return jnp.dot(
            weights, values, preferred_element_type=jnp.float32, precision=lax.Precision.HIGHEST
        )

    return lax.map(apply_block, grouped).reshape(row_count, values.shape[1])


def squares(residual):
    return lax.psum(jnp.sum(residual * residual, axis=0), AXES)


def blockwise(positions, radii, right_side):
    local_count = positions.shape[1]
    total = local_count * lax.axis_size("row") * lax.axis_size("col")
    kernel_scale, softening = constants(total)
    row_points = lax.all_gather(positions, "col", axis=1, tiled=True)
    col_points = lax.all_gather(positions, "row", axis=1, tiled=True)
    limit = 1 << 20
    solution = jnp.zeros_like(right_side)
    residual = right_side
    direction = right_side
    norm_now = squares(residual)
    for iteration in range(ITERS):
        col_values = lax.all_gather(direction, "row", axis=0, tiled=True)
        summed = lax.psum_scatter(
            kernel_product(row_points, col_points, col_values, kernel_scale, softening, limit),
            "col",
            scatter_dimension=0,
            tiled=True,
        )
        image_vec = direction / radii[:, None] + summed
        curvature = lax.psum(jnp.sum(direction * image_vec, axis=0), AXES)
        step_size = norm_now / curvature
        solution = solution + step_size * direction
        residual = residual - step_size * image_vec
        if iteration + 1 < ITERS:
            norm_next = squares(residual)
            direction = residual + norm_next / norm_now * direction
            norm_now = norm_next
    return (solution, residual)


def pack_kernel(scale, parts, pos_ref, rad_ref, rhs_ref, out_ref):
    cols = rhs_ref.shape[1] // parts
    flipped = rhs_ref[...].T
    extra = jnp.concatenate(
        [pos_ref[...] * scale, rad_ref[...], jnp.zeros((EXTRA - 4, LANES), F32)], axis=0
    )
    for q in range(parts):
        out_ref[q, 0:cols, :] = flipped[q * cols : (q + 1) * cols, :]
        out_ref[q, cols : cols + EXTRA, :] = extra


def split(values):
    high = values.astype(BF16)
    return high, (values - high.astype(F32)).astype(BF16)


def first_kernel(soft, own_ref, oth_ref, *refs):
    pieces = (len(refs) - 4) // 2
    highs, lows = refs[0:pieces], refs[pieces : 2 * pieces]
    image_ref, lane_ref, sub_ref, vec_ref = refs[2 * pieces :]
    parts, cols = own_ref.shape[0], own_ref.shape[1] - EXTRA
    half = parts * LANES
    for h, ref in enumerate((own_ref, oth_ref)):
        for q in range(parts):
            at = slice(h * half + q * LANES, h * half + (q + 1) * LANES)
            high, low = split(ref[q, 0:cols, :])
            vec_ref[0:cols, at] = high
            vec_ref[cols : 2 * cols, at] = low
            extra = ref[q, cols : cols + EXTRA, :]
            if h == 0:
                lane_ref[:, at] = extra
            turned = extra.T
            for c in range(3):
                sub_ref[c, at, :] = jnp.broadcast_to(turned[:, c : c + 1], (LANES, LANES))
    wide, deep, step = 512, 1024, 256
    width = highs[0].shape[1]
    for piece in range(pieces):
        high_ref, low_ref = highs[piece], lows[piece]

        def tile(t, _, piece=piece, high_ref=high_ref, low_ref=low_ref):
            i0 = pl.multiple_of(t * wide, wide)
            here = pl.ds(pl.multiple_of(piece * width + t * wide, wide), wide)
            ends = [lane_ref[c : c + 1, here] for c in range(3)]

            def rows(u, acc):
                for r in range(0, deep, step):
                    at = pl.ds(pl.multiple_of(u * deep + r, step), step)
                    starts = [sub_ref[c, at, :] for c in range(3)]
                    high, low = [], []
                    for s in range(0, wide, LANES):
                        gaps = [starts[c] - ends[c][:, s : s + LANES] for c in range(3)]
                        squared = gaps[0] * gaps[0] + gaps[1] * gaps[1] + gaps[2] * gaps[2]
                        a, b = split(lax.rsqrt(squared + soft))
                        high.append(a)
                        low.append(b)
                    high, low = jnp.concatenate(high, 1), jnp.concatenate(low, 1)
                    high_ref[at, pl.ds(i0, wide)] = high
                    low_ref[at, pl.ds(i0, wide)] = low
                    vec = vec_ref[:, at]
                    acc = acc + jnp.dot(vec, high, preferred_element_type=F32)
                    acc = acc + jnp.dot(vec, low, preferred_element_type=F32)
                return acc

            acc = lax.fori_loop(0, 2 * half // deep, rows, jnp.zeros((2 * cols, wide), F32))
            image_ref[:, here] = acc[0:cols] + acc[cols : 2 * cols]
            return 0

        lax.fori_loop(0, width // wide, tile, 0)
    for q in range(parts):
        at = slice(q * LANES, (q + 1) * LANES)
        image_ref[:, at] = image_ref[:, at] + own_ref[q, 0:cols, :] / lane_ref[3:4, at]


def second_kernel(own_ref, oth_ref, im_own_ref, im_oth_ref, *refs):
    pieces = (len(refs) - 5) // 2
    highs, lows = refs[0:pieces], refs[pieces : 2 * pieces]
    dir_ref, res_ref, image_ref, stat_ref, vec_ref = refs[2 * pieces :]
    parts, cols = own_ref.shape[0], own_ref.shape[1] - EXTRA
    half = parts * LANES
    blocks = [
        (rhs, im, q, slice(q * LANES, (q + 1) * LANES), slice(h * half + q * LANES, h * half + (q + 1) * LANES))
        for h, (rhs, im) in enumerate(((own_ref, im_own_ref), (oth_ref, im_oth_ref)))
        for q in range(parts)
    ]
    norm, curve = jnp.zeros((cols, LANES), F32), jnp.zeros((cols, LANES), F32)
    for rhs, im, q, at, _ in blocks:
        value = rhs[q, 0:cols, :]
        norm = norm + value * value
        curve = curve + value * im[:, at]
    norm = jnp.sum(norm, axis=1, keepdims=True)
    step = norm / jnp.sum(curve, axis=1, keepdims=True)
    fresh = jnp.zeros((cols, LANES), F32)
    for rhs, im, q, at, _ in blocks:
        value = rhs[q, 0:cols, :] - step * im[:, at]
        fresh = fresh + value * value
    fresh = jnp.sum(fresh, axis=1, keepdims=True)
    ratio = fresh / norm
    for n, (rhs, im, q, at, to) in enumerate(blocks):
        value = rhs[q, 0:cols, :]
        left = value - step * im[:, at]
        direction = left + ratio * value
        if n < parts:
            res_ref[:, at] = left
            dir_ref[:, at] = direction
        high, low = split(direction)
        vec_ref[0:cols, to] = high
        vec_ref[cols : 2 * cols, to] = low
    width = highs[0].shape[1]
    deep = 256
    for piece in range(pieces):
        acc = jnp.zeros((2 * cols, width), F32)
        for r in range(0, 2 * half, deep):
            vec = vec_ref[:, r : r + deep]
            acc = acc + jnp.dot(vec, highs[piece][r : r + deep, :], preferred_element_type=F32)
            acc = acc + jnp.dot(vec, lows[piece][r : r + deep, :], preferred_element_type=F32)
        image_ref[:, piece * width : (piece + 1) * width] = acc[0:cols] + acc[cols : 2 * cols]
    curve = jnp.zeros((cols, LANES), F32)
    for q in range(parts):
        at = slice(q * LANES, (q + 1) * LANES)
        direction = dir_ref[:, at]
        image = image_ref[:, at] + direction / own_ref[q, cols + 3 : cols + 4, :]
        image_ref[:, at] = image
        curve = curve + direction * image
    stat_ref[0] = curve
    stat_ref[1] = jnp.broadcast_to(step, (cols, LANES))
    stat_ref[2] = jnp.broadcast_to(fresh, (cols, LANES))


def last_kernel(own_ref, dir_ref, res_ref, image_ref, stat_ref, curve_ref, out_ref):
    parts, cols = own_ref.shape[0], own_ref.shape[1] - EXTRA
    curve = jnp.sum(stat_ref[0] + curve_ref[...], axis=1, keepdims=True)
    first = stat_ref[1, :, 0:1]
    step = stat_ref[2, :, 0:1] / curve
    for q in range(parts):
        at = slice(q * LANES, (q + 1) * LANES)
        out_ref[q, 0:cols, :] = first * own_ref[q, 0:cols, :] + step * dir_ref[:, at]
        out_ref[q, cols : 2 * cols, :] = res_ref[:, at] - step * image_ref[:, at]


def unpack_kernel(in_ref, sol_ref, res_ref):
    parts, cols = in_ref.shape[0], in_ref.shape[1] // 2
    sol_ref[...] = in_ref[:, 0:cols, :].reshape(parts * cols, LANES).T
    res_ref[...] = in_ref[:, cols : 2 * cols, :].reshape(parts * cols, LANES).T


def shape(*dims, dtype=F32):
    return jax.ShapeDtypeStruct(dims, dtype)


def call(kernel, out, count, scratch=(), limit=16):
    many = isinstance(out, (list, tuple))
    return pl.pallas_call(
        kernel,
        out_shape=out,
        in_specs=[VM] * count,
        out_specs=[VM] * len(out) if many else VM,
        scratch_shapes=list(scratch),
        compiler_params=pltpu.CompilerParams(vmem_limit_bytes=limit << 20),
    )


def by_columns(positions, radii, right_side):
    row_size, col_size = lax.axis_size("row"), lax.axis_size("col")
    devices = row_size * col_size
    parts = devices // 2
    total = right_side.shape[0] * devices
    cols = right_side.shape[1] // parts
    half = total // 2
    kernel_scale, softening = constants(total)
    soft = softening / (kernel_scale * kernel_scale)
    groups = [[2 * chip + core for chip in range(parts)] for core in range(2)]
    swap = [(i, i ^ 1) for i in range(col_size)]
    pieces = 2

    packed = call(functools.partial(pack_kernel, 1.0 / kernel_scale, parts), shape(parts, cols + EXTRA, LANES), 3)(
        positions, radii.reshape(1, -1), right_side
    )
    own = lax.all_to_all(packed, AXES, 0, 0, axis_index_groups=groups, tiled=True)
    oth = lax.ppermute(own, "col", swap)
    *kernel, image = call(
        functools.partial(first_kernel, soft),
        [shape(total, half // pieces, dtype=BF16)] * (2 * pieces) + [shape(cols, half)],
        2,
        [
            pltpu.VMEM((EXTRA, half), F32),
            pltpu.VMEM((3, total, LANES), F32),
            pltpu.VMEM((2 * cols, total), BF16),
        ],
    )(own, oth)
    direction, residual, image, stats = call(
        second_kernel,
        [shape(cols, half)] * 3 + [shape(3, cols, LANES)],
        4 + 2 * pieces,
        [pltpu.VMEM((2 * cols, total), BF16)],
    )(own, oth, image, lax.ppermute(image, "col", swap), *kernel)
    curve = lax.ppermute(stats[0], "col", swap)
    mixed = call(last_kernel, shape(parts, 2 * cols, LANES), 6)(own, direction, residual, image, stats, curve)
    mixed = lax.all_to_all(mixed, AXES, 0, 0, axis_index_groups=groups, tiled=True)
    return tuple(call(unpack_kernel, [shape(LANES, parts * cols)] * 2, 1)(mixed))


def body(positions, radii, right_side):
    devices = lax.axis_size("row") * lax.axis_size("col")
    rows, columns = right_side.shape
    total = rows * devices
    fits = rows == LANES and devices % 2 == 0 and columns % (devices // 2) == 0
    if fits and columns // (devices // 2) == 16 and 2 * total * total <= KERNEL_BYTES:
        return by_columns(positions, radii, right_side)
    return blockwise(positions, radii, right_side)


def solution(mesh):
    return jax.shard_map(
        body,
        mesh=mesh,
        in_specs=(P(None, ("row", "col")), P(("row", "col")), P(("row", "col"), None)),
        out_specs=(P(("row", "col"), None), P(("row", "col"), None)),
        check_vma=False,
    )
```

```python
import functools

import jax
import jax.numpy as jnp
from jax import lax
from jax.experimental import pallas as pl
from jax.experimental.pallas import tpu as pltpu
from jax.sharding import PartitionSpec as P

ITERS = 2
AXES = ("row", "col")
F32 = jnp.float32
BF16 = jnp.bfloat16
LANES = 128
EXTRA = 8
PANEL = 256
WIDE = 512
VM = pl.BlockSpec(memory_space=pltpu.VMEM)
SM = pl.BlockSpec(memory_space=pltpu.SMEM)
KERNEL_BYTES = 32 << 20


def constants(total):
    kernel_scale = float(total) ** (-0.5)
    spacing = 0.25 * float(total) ** (-1.0 / 3.0)
    return (kernel_scale, spacing * spacing)


def kernel_product(row_points, col_points, values, kernel_scale, softening, limit):
    row_count = row_points.shape[1]
    col_count = col_points.shape[1]
    blocks = max(1, row_count * col_count // limit)
    while row_count % blocks:
        blocks = blocks - 1
    block_size = row_count // blocks
    grouped = row_points.reshape(3, blocks, block_size).transpose(1, 0, 2)

    def apply_block(row_block):
        first = row_block[0][:, None] - col_points[0][None, :]
        second = row_block[1][:, None] - col_points[1][None, :]
        third = row_block[2][:, None] - col_points[2][None, :]
        squared = first * first + second * second + third * third
        weights = lax.rsqrt(squared + softening) * kernel_scale
        return jnp.dot(
            weights, values, preferred_element_type=jnp.float32, precision=lax.Precision.HIGHEST
        )

    return lax.map(apply_block, grouped).reshape(row_count, values.shape[1])


def squares(residual):
    return lax.psum(jnp.sum(residual * residual, axis=0), AXES)


def blockwise(positions, radii, right_side):
    local_count = positions.shape[1]
    total = local_count * lax.axis_size("row") * lax.axis_size("col")
    kernel_scale, softening = constants(total)
    row_points = lax.all_gather(positions, "col", axis=1, tiled=True)
    col_points = lax.all_gather(positions, "row", axis=1, tiled=True)
    limit = 1 << 20
    solution = jnp.zeros_like(right_side)
    residual = right_side
    direction = right_side
    norm_now = squares(residual)
    for iteration in range(ITERS):
        col_values = lax.all_gather(direction, "row", axis=0, tiled=True)
        summed = lax.psum_scatter(
            kernel_product(row_points, col_points, col_values, kernel_scale, softening, limit),
            "col",
            scatter_dimension=0,
            tiled=True,
        )
        image_vec = direction / radii[:, None] + summed
        curvature = lax.psum(jnp.sum(direction * image_vec, axis=0), AXES)
        step_size = norm_now / curvature
        solution = solution + step_size * direction
        residual = residual - step_size * image_vec
        if iteration + 1 < ITERS:
            norm_next = squares(residual)
            direction = residual + norm_next / norm_now * direction
            norm_now = norm_next
    return (solution, residual)


def pack_kernel(scale, parts, pos_hbm, rad_hbm, rhs_hbm, out_ref, pos_ref, rad_ref, rhs_ref, sems):
    copies = [
        pltpu.make_async_copy(src, dst, sems.at[n])
        for n, (src, dst) in enumerate(((rhs_hbm, rhs_ref), (pos_hbm, pos_ref), (rad_hbm, rad_ref)))
    ]
    for copy in copies:
        copy.start()
    for copy in copies:
        copy.wait()
    cols = rhs_ref.shape[1] // parts
    flipped = rhs_ref[...].T
    extra = jnp.concatenate(
        [pos_ref[...] * scale, rad_ref[...], jnp.zeros((EXTRA - 4, LANES), F32)], axis=0
    )
    for q in range(parts):
        out_ref[q, 0:cols, :] = flipped[q * cols : (q + 1) * cols, :]
        out_ref[q, cols : cols + EXTRA, :] = extra


def split(values):
    high = values.astype(BF16)
    return high, (values - high.astype(F32)).astype(BF16)


def product(vec, high, low):
    return jnp.dot(vec, high, preferred_element_type=F32) + jnp.dot(vec, low, preferred_element_type=F32)


def evaluate(soft, sub_ref, rows, lane_ref, at):
    starts = [sub_ref[c, rows, :] for c in range(3)]
    ends = [lane_ref[c : c + 1, at] for c in range(3)]
    high, low = [], []
    for s in range(0, ends[0].shape[1], LANES):
        gaps = [starts[c] - ends[c][:, s : s + LANES] for c in range(3)]
        squared = gaps[0] * gaps[0] + gaps[1] * gaps[1] + gaps[2] * gaps[2]
        a, b = split(lax.rsqrt(squared + soft))
        high.append(a)
        low.append(b)
    return jnp.concatenate(high, 1), jnp.concatenate(low, 1)


def unpack(ref, lane_ref, vec_ref, sub_ref=None):
    parts, cols = ref.shape[0], ref.shape[1] - EXTRA
    for q in range(parts):
        at = slice(q * LANES, (q + 1) * LANES)
        high, low = split(ref[q, 0:cols, :])
        vec_ref[0:cols, at] = high
        vec_ref[cols : 2 * cols, at] = low
        extra = ref[q, cols : cols + EXTRA, :]
        lane_ref[:, at] = extra
        if sub_ref is not None:
            turned = extra.T
            for c in range(3):
                sub_ref[c, at, :] = jnp.broadcast_to(turned[:, c : c + 1], (LANES, LANES))


def near_spans(panels):
    spans, start = [], 0
    for t in range(panels):
        spans.append((t, slice(t * PANEL, panels * PANEL), start))
        start += (panels - t) * PANEL
    return spans


def across_spans(panels):
    spans, start = [], 0
    for t in range(1, panels):
        spans.append((t, slice(0, t * PANEL), start))
        start += t * PANEL
    return spans


def first_kernel(soft, own_ref, high_ref, low_ref, high_t_ref, low_t_ref, vec_ref, sub_ref, acc_ref, lane_ref):
    panels = vec_ref.shape[1] // PANEL
    unpack(own_ref, lane_ref, vec_ref, sub_ref)
    acc_ref[...] = jnp.zeros_like(acc_ref)
    for t, columns, start in near_spans(panels):
        rows = slice(t * PANEL, (t + 1) * PANEL)
        for c in range(columns.start, columns.stop, WIDE):
            at = slice(c, min(c + WIDE, columns.stop))
            high, low = evaluate(soft, sub_ref, rows, lane_ref, at)
            to = start + c - columns.start
            high_ref[:, to : to + at.stop - c] = high
            low_ref[:, to : to + at.stop - c] = low
            acc_ref[:, at] += product(vec_ref[:, rows], high, low)
            skip = PANEL if c == columns.start else 0
            if at.stop - c > skip:
                high, low = high[:, skip:].T, low[:, skip:].T
                to = to + skip - (t + 1) * PANEL
                high_t_ref[to : to + at.stop - c - skip, :] = high
                low_t_ref[to : to + at.stop - c - skip, :] = low
                acc_ref[:, rows] += product(vec_ref[:, c + skip : at.stop], high, low)


def middle_kernel(soft, core_ref, own_ref, oth_ref, vec_ref, sub_ref, near_ref, *refs):
    high_ref, low_ref, high_t_ref, low_t_ref, far_ref, image_ref, acc_ref, lane_ref, vec_oth_ref = refs
    parts, cols = own_ref.shape[0], own_ref.shape[1] - EXTRA
    half = parts * LANES
    panels = half // PANEL
    unpack(oth_ref, lane_ref, vec_oth_ref)
    acc_ref[:, 0:half] = near_ref[...]
    acc_ref[:, half:] = jnp.zeros_like(near_ref)
    for t, columns, start in across_spans(panels):
        rows = slice(t * PANEL, (t + 1) * PANEL)
        for c in range(columns.start, columns.stop, WIDE):
            at = slice(c, min(c + WIDE, columns.stop))
            high, low = evaluate(soft, sub_ref, rows, lane_ref, at)
            to = slice(start + c, start + at.stop)
            high_ref[:, to] = high
            low_ref[:, to] = low
            acc_ref[:, half + c : half + at.stop] += product(vec_ref[:, rows], high, low)
            high, low = high.T, low.T
            high_t_ref[to, :] = high
            low_t_ref[to, :] = low
            acc_ref[:, rows] += product(vec_oth_ref[:, at], high, low)
    for n in range(panels // 2):
        place = pl.multiple_of((core_ref[0] * (panels // 2) + n) * PANEL, PANEL)
        rows, at = pl.ds(place, PANEL), pl.ds(pl.multiple_of(half + place, PANEL), PANEL)
        high, low = evaluate(soft, sub_ref, rows, lane_ref, rows)
        far_ref[n, 0] = high
        far_ref[n, 1] = low
        acc_ref[:, at] += product(vec_ref[:, rows], high, low)
        high, low = high.T, low.T
        far_ref[n, 2] = high
        far_ref[n, 3] = low
        acc_ref[:, rows] += product(vec_oth_ref[:, rows], high, low)
    for q in range(parts):
        at = slice(q * LANES, (q + 1) * LANES)
        here = own_ref[q, 0:cols, :] / own_ref[q, cols + 3 : cols + 4, :]
        image_ref[:, at] = acc_ref[0:cols, at] + acc_ref[cols : 2 * cols, at] + here
    image_ref[:, half:] = acc_ref[0:cols, half:] + acc_ref[cols : 2 * cols, half:]


def second_kernel(core_ref, own_ref, oth_ref, mine_ref, theirs_ref, *refs):
    near, across, far_ref = refs[0:4], refs[4:8], refs[8]
    dir_ref, res_ref, image_ref, send_ref, stat_ref, vec_ref, acc_ref, sum_ref = refs[9:]
    parts, cols = own_ref.shape[0], own_ref.shape[1] - EXTRA
    half = parts * LANES
    panels = half // PANEL
    sum_ref[:, 0:half] = mine_ref[:, 0:half] + theirs_ref[:, half:]
    sum_ref[:, half:] = mine_ref[:, half:] + theirs_ref[:, 0:half]
    blocks = [
        (ref, q, slice(h * half + q * LANES, h * half + (q + 1) * LANES))
        for h, ref in enumerate((own_ref, oth_ref))
        for q in range(parts)
    ]
    zero = jnp.zeros((cols, LANES), F32)
    norm, curve, fresh = zero, zero, zero
    for ref, q, at in blocks:
        value = ref[q, 0:cols, :]
        norm = norm + value * value
        curve = curve + value * sum_ref[:, at]
    norm = jnp.sum(norm, axis=1, keepdims=True)
    step = norm / jnp.sum(curve, axis=1, keepdims=True)
    for ref, q, at in blocks:
        value = ref[q, 0:cols, :] - step * sum_ref[:, at]
        fresh = fresh + value * value
    fresh = jnp.sum(fresh, axis=1, keepdims=True)
    ratio = fresh / norm
    for n, (ref, q, at) in enumerate(blocks):
        value = ref[q, 0:cols, :]
        left = value - step * sum_ref[:, at]
        direction = left + ratio * value
        if n < parts:
            res_ref[:, at] = left
        dir_ref[:, at] = direction
        high, low = split(direction)
        vec_ref[0:cols, at] = high
        vec_ref[cols : 2 * cols, at] = low
    acc_ref[...] = jnp.zeros_like(acc_ref)
    for t, columns, start in near_spans(panels):
        rows, after = slice(t * PANEL, (t + 1) * PANEL), slice((t + 1) * PANEL, half)
        to = slice(start, start + half - rows.start)
        acc_ref[:, columns] += product(vec_ref[:, rows], near[0][:, to], near[1][:, to])
        if after.start < half:
            to = slice(start - rows.start, start - rows.start + half - after.start)
            acc_ref[:, rows] += product(vec_ref[:, after], near[2][to, :], near[3][to, :])
    for t, columns, start in across_spans(panels):
        rows, there = slice(t * PANEL, (t + 1) * PANEL), slice(half, half + columns.stop)
        to = slice(start, start + columns.stop)
        acc_ref[:, there] += product(vec_ref[:, rows], across[0][:, to], across[1][:, to])
        acc_ref[:, rows] += product(vec_ref[:, there], across[2][to, :], across[3][to, :])
    for n in range(panels // 2):
        place = pl.multiple_of((core_ref[0] * (panels // 2) + n) * PANEL, PANEL)
        rows, at = pl.ds(place, PANEL), pl.ds(pl.multiple_of(half + place, PANEL), PANEL)
        acc_ref[:, at] += product(vec_ref[:, rows], far_ref[n, 0], far_ref[n, 1])
        acc_ref[:, rows] += product(vec_ref[:, at], far_ref[n, 2], far_ref[n, 3])
    curve = zero
    for n, (ref, q, at) in enumerate(blocks):
        direction = dir_ref[:, at]
        image = acc_ref[0:cols, at] + acc_ref[cols : 2 * cols, at]
        if n < parts:
            image = image + direction / own_ref[q, cols + 3 : cols + 4, :]
            image_ref[:, at] = image
        else:
            send_ref[:, at.start - half : at.stop - half] = image
        curve = curve + direction * image
    send_ref[:, half:] = curve
    stat_ref[0] = jnp.broadcast_to(step, (cols, LANES))
    stat_ref[1] = jnp.broadcast_to(fresh, (cols, LANES))


def last_kernel(own_ref, dir_ref, res_ref, image_ref, send_ref, come_ref, stat_ref, out_ref):
    parts, cols = own_ref.shape[0], own_ref.shape[1] - EXTRA
    half = parts * LANES
    curve = jnp.sum(send_ref[:, half:] + come_ref[:, half:], axis=1, keepdims=True)
    first = stat_ref[0, :, 0:1]
    step = stat_ref[1, :, 0:1] / curve
    for q in range(parts):
        at = slice(q * LANES, (q + 1) * LANES)
        out_ref[q, 0:cols, :] = first * own_ref[q, 0:cols, :] + step * dir_ref[:, at]
        out_ref[q, cols : 2 * cols, :] = res_ref[:, at] - step * (image_ref[:, at] + come_ref[:, at])


def unpack_kernel(in_ref, sol_ref, res_ref):
    parts, cols = in_ref.shape[0], in_ref.shape[1] // 2
    sol_ref[...] = in_ref[:, 0:cols, :].reshape(parts * cols, LANES).T
    res_ref[...] = in_ref[:, cols : 2 * cols, :].reshape(parts * cols, LANES).T


def shape(*dims, dtype=F32):
    return jax.ShapeDtypeStruct(dims, dtype)


def call(kernel, out, ins, scratch=(), limit=8):
    return pl.pallas_call(
        kernel,
        out_shape=out,
        in_specs=ins,
        out_specs=[VM] * len(out),
        scratch_shapes=list(scratch),
        compiler_params=pltpu.CompilerParams(vmem_limit_bytes=limit << 20),
    )


def by_columns(positions, radii, right_side):
    row_size, col_size = lax.axis_size("row"), lax.axis_size("col")
    devices = row_size * col_size
    parts = devices // 2
    rows, columns = right_side.shape
    total = rows * devices
    cols = columns // parts
    half = total // 2
    panels = half // PANEL
    kernel_scale, softening = constants(total)
    soft = softening / (kernel_scale * kernel_scale)
    groups = [[2 * chip + core for chip in range(parts)] for core in range(2)]
    swap = [(i, i ^ 1) for i in range(col_size)]
    core = (lax.axis_index("col") % 2).astype(jnp.int32).reshape(1)

    (packed,) = call(
        functools.partial(pack_kernel, 1.0 / kernel_scale, parts),
        [shape(parts, cols + EXTRA, LANES)],
        [pl.BlockSpec(memory_space=pltpu.HBM)] * 3,
        [
            pltpu.VMEM((3, LANES), F32),
            pltpu.VMEM((1, LANES), F32),
            pltpu.VMEM((LANES, columns), F32),
            pltpu.SemaphoreType.DMA((3,)),
        ],
        60,
    )(positions, radii.reshape(1, -1), right_side)
    own = lax.all_to_all(packed, AXES, 0, 0, axis_index_groups=groups, tiled=True)
    oth = lax.ppermute(own, "col", swap)
    sizes = [sum(cs.stop - cs.start for _, cs, _ in spans(panels)) for spans in (near_spans, across_spans)]
    *near, vec, sub, acc = call(
        functools.partial(first_kernel, soft),
        [shape(PANEL, sizes[0], dtype=BF16)] * 2
        + [shape(sizes[0] - half, PANEL, dtype=BF16)] * 2
        + [shape(2 * cols, half, dtype=BF16), shape(3, half, LANES), shape(2 * cols, half)],
        [VM],
        [pltpu.VMEM((EXTRA, half), F32)],
        16,
    )(own)
    *across, mine = call(
        functools.partial(middle_kernel, soft),
        [shape(PANEL, sizes[1], dtype=BF16)] * 2
        + [shape(sizes[1], PANEL, dtype=BF16)] * 2
        + [shape(panels // 2, 4, PANEL, PANEL, dtype=BF16), shape(cols, total)],
        [SM] + [VM] * 5,
        [
            pltpu.VMEM((2 * cols, total), F32),
            pltpu.VMEM((EXTRA, half), F32),
            pltpu.VMEM((2 * cols, half), BF16),
        ],
        16,
    )(core, own, oth, vec, sub, acc)
    direction, residual, image, send, stats = call(
        second_kernel,
        [shape(cols, total), shape(cols, half), shape(cols, half), shape(cols, half + LANES), shape(2, cols, LANES)],
        [SM] + [VM] * 13,
        [
            pltpu.VMEM((2 * cols, total), BF16),
            pltpu.VMEM((2 * cols, total), F32),
            pltpu.VMEM((cols, total), F32),
        ],
    )(core, own, oth, mine, lax.ppermute(mine, "col", swap), *near, *across)
    come = lax.ppermute(send, "col", swap)
    (mixed,) = call(last_kernel, [shape(parts, 2 * cols, LANES)], [VM] * 7)(
        own, direction, residual, image, send, come, stats
    )
    mixed = lax.all_to_all(mixed, AXES, 0, 0, axis_index_groups=groups, tiled=True)
    return tuple(call(unpack_kernel, [shape(LANES, columns)] * 2, [VM])(mixed))


def body(positions, radii, right_side):
    devices = lax.axis_size("row") * lax.axis_size("col")
    rows, columns = right_side.shape
    total = rows * devices
    fits = rows == LANES and total % (4 * PANEL) == 0 and 16 * devices == 2 * columns
    if fits and 2 * total * total <= KERNEL_BYTES:
        return by_columns(positions, radii, right_side)
    return blockwise(positions, radii, right_side)


def solution(mesh):
    return jax.shard_map(
        body,
        mesh=mesh,
        in_specs=(P(None, ("row", "col")), P(("row", "col")), P(("row", "col"), None)),
        out_specs=(P(("row", "col"), None), P(("row", "col"), None)),
        check_vma=False,
    )
```

```python
import functools

import jax
import jax.numpy as jnp
from jax import lax
from jax.experimental import pallas as pl
from jax.experimental.pallas import tpu as pltpu
from jax.sharding import PartitionSpec as P

ITERS = 2
AXES = ("row", "col")
F32 = jnp.float32
BF16 = jnp.bfloat16
LANES = 128
EXTRA = 8
PANEL = 256
WIDE = 512
VM = pl.BlockSpec(memory_space=pltpu.VMEM)
SM = pl.BlockSpec(memory_space=pltpu.SMEM)
KERNEL_BYTES = 32 << 20


def constants(total):
    kernel_scale = float(total) ** (-0.5)
    spacing = 0.25 * float(total) ** (-1.0 / 3.0)
    return (kernel_scale, spacing * spacing)


def kernel_product(row_points, col_points, values, kernel_scale, softening, limit):
    row_count = row_points.shape[1]
    col_count = col_points.shape[1]
    blocks = max(1, row_count * col_count // limit)
    while row_count % blocks:
        blocks = blocks - 1
    block_size = row_count // blocks
    grouped = row_points.reshape(3, blocks, block_size).transpose(1, 0, 2)

    def apply_block(row_block):
        first = row_block[0][:, None] - col_points[0][None, :]
        second = row_block[1][:, None] - col_points[1][None, :]
        third = row_block[2][:, None] - col_points[2][None, :]
        squared = first * first + second * second + third * third
        weights = lax.rsqrt(squared + softening) * kernel_scale
        return jnp.dot(
            weights, values, preferred_element_type=jnp.float32, precision=lax.Precision.HIGHEST
        )

    return lax.map(apply_block, grouped).reshape(row_count, values.shape[1])


def squares(residual):
    return lax.psum(jnp.sum(residual * residual, axis=0), AXES)


def blockwise(positions, radii, right_side):
    local_count = positions.shape[1]
    total = local_count * lax.axis_size("row") * lax.axis_size("col")
    kernel_scale, softening = constants(total)
    row_points = lax.all_gather(positions, "col", axis=1, tiled=True)
    col_points = lax.all_gather(positions, "row", axis=1, tiled=True)
    limit = 1 << 20
    solution = jnp.zeros_like(right_side)
    residual = right_side
    direction = right_side
    norm_now = squares(residual)
    for iteration in range(ITERS):
        col_values = lax.all_gather(direction, "row", axis=0, tiled=True)
        summed = lax.psum_scatter(
            kernel_product(row_points, col_points, col_values, kernel_scale, softening, limit),
            "col",
            scatter_dimension=0,
            tiled=True,
        )
        image_vec = direction / radii[:, None] + summed
        curvature = lax.psum(jnp.sum(direction * image_vec, axis=0), AXES)
        step_size = norm_now / curvature
        solution = solution + step_size * direction
        residual = residual - step_size * image_vec
        if iteration + 1 < ITERS:
            norm_next = squares(residual)
            direction = residual + norm_next / norm_now * direction
            norm_now = norm_next
    return (solution, residual)


def pack_kernel(scale, parts, pos_hbm, rad_hbm, rhs_hbm, out_ref, pos_ref, rad_ref, rhs_ref, sems):
    copies = [
        pltpu.make_async_copy(src, dst, sems.at[n])
        for n, (src, dst) in enumerate(((rhs_hbm, rhs_ref), (pos_hbm, pos_ref), (rad_hbm, rad_ref)))
    ]
    for copy in copies:
        copy.start()
    for copy in copies:
        copy.wait()
    cols = rhs_ref.shape[1] // parts
    flipped = rhs_ref[...].T
    extra = jnp.concatenate(
        [pos_ref[...] * scale, rad_ref[...], jnp.zeros((EXTRA - 4, LANES), F32)], axis=0
    )
    for q in range(parts):
        out_ref[q, 0:cols, :] = flipped[q * cols : (q + 1) * cols, :]
        out_ref[q, cols : cols + EXTRA, :] = extra


def split(values):
    high = values.astype(BF16)
    return high, (values - high.astype(F32)).astype(BF16)


def product(vec, high, low):
    return jnp.dot(vec, high, preferred_element_type=F32) + jnp.dot(vec, low, preferred_element_type=F32)


def evaluate(soft, sub_ref, rows, lane_ref, at):
    starts = [sub_ref[c, rows, :] for c in range(3)]
    ends = [lane_ref[c : c + 1, at] for c in range(3)]
    high, low = [], []
    for s in range(0, ends[0].shape[1], LANES):
        gaps = [starts[c] - ends[c][:, s : s + LANES] for c in range(3)]
        squared = gaps[0] * gaps[0] + gaps[1] * gaps[1] + gaps[2] * gaps[2]
        a, b = split(lax.rsqrt(squared + soft))
        high.append(a)
        low.append(b)
    return jnp.concatenate(high, 1), jnp.concatenate(low, 1)


def unpack(ref, lane_ref, vec_ref, sub_ref=None):
    parts, cols = ref.shape[0], ref.shape[1] - EXTRA
    for q in range(parts):
        at = slice(q * LANES, (q + 1) * LANES)
        high, low = split(ref[q, 0:cols, :])
        vec_ref[0:cols, at] = high
        vec_ref[cols : 2 * cols, at] = low
        extra = ref[q, cols : cols + EXTRA, :]
        lane_ref[:, at] = extra
        if sub_ref is not None:
            turned = extra.T
            for c in range(3):
                sub_ref[c, at, :] = jnp.broadcast_to(turned[:, c : c + 1], (LANES, LANES))


def near_spans(panels):
    spans, start = [], 0
    for t in range(panels):
        spans.append((t, slice(t * PANEL, panels * PANEL), start))
        start += (panels - t) * PANEL
    return spans


def across_spans(panels):
    spans, start = [], 0
    for t in range(1, panels):
        spans.append((t, slice(0, t * PANEL), start))
        start += t * PANEL
    return spans


def first_kernel(soft, own_ref, high_ref, low_ref, high_t_ref, low_t_ref, vec_ref, sub_ref, acc_ref, lane_ref):
    panels = vec_ref.shape[1] // PANEL
    unpack(own_ref, lane_ref, vec_ref, sub_ref)
    acc_ref[...] = jnp.zeros_like(acc_ref)
    for t, columns, start in near_spans(panels):
        rows = slice(t * PANEL, (t + 1) * PANEL)
        for c in range(columns.start, columns.stop, WIDE):
            at = slice(c, min(c + WIDE, columns.stop))
            high, low = evaluate(soft, sub_ref, rows, lane_ref, at)
            to = start + c - columns.start
            high_ref[:, to : to + at.stop - c] = high
            low_ref[:, to : to + at.stop - c] = low
            acc_ref[:, at] += product(vec_ref[:, rows], high, low)
            skip = PANEL if c == columns.start else 0
            if at.stop - c > skip:
                high, low = high[:, skip:].T, low[:, skip:].T
                to = to + skip - (t + 1) * PANEL
                high_t_ref[to : to + at.stop - c - skip, :] = high
                low_t_ref[to : to + at.stop - c - skip, :] = low
                acc_ref[:, rows] += product(vec_ref[:, c + skip : at.stop], high, low)


def middle_kernel(soft, core_ref, own_ref, oth_ref, vec_ref, sub_ref, near_ref, *refs):
    high_ref, low_ref, high_t_ref, low_t_ref, far_ref, image_ref, acc_ref, lane_ref, vec_oth_ref = refs
    parts, cols = own_ref.shape[0], own_ref.shape[1] - EXTRA
    half = parts * LANES
    panels = half // PANEL
    unpack(oth_ref, lane_ref, vec_oth_ref)
    acc_ref[:, 0:half] = near_ref[...]
    acc_ref[:, half:] = jnp.zeros_like(near_ref)
    for t, columns, start in across_spans(panels):
        rows = slice(t * PANEL, (t + 1) * PANEL)
        for c in range(columns.start, columns.stop, WIDE):
            at = slice(c, min(c + WIDE, columns.stop))
            high, low = evaluate(soft, sub_ref, rows, lane_ref, at)
            to = slice(start + c, start + at.stop)
            high_ref[:, to] = high
            low_ref[:, to] = low
            acc_ref[:, half + c : half + at.stop] += product(vec_ref[:, rows], high, low)
            high, low = high.T, low.T
            high_t_ref[to, :] = high
            low_t_ref[to, :] = low
            acc_ref[:, rows] += product(vec_oth_ref[:, at], high, low)
    for n in range(panels // 2):
        place = pl.multiple_of((core_ref[0] * (panels // 2) + n) * PANEL, PANEL)
        rows, at = pl.ds(place, PANEL), pl.ds(pl.multiple_of(half + place, PANEL), PANEL)
        high, low = evaluate(soft, sub_ref, rows, lane_ref, rows)
        far_ref[n, 0] = high
        far_ref[n, 1] = low
        acc_ref[:, at] += product(vec_ref[:, rows], high, low)
        high, low = high.T, low.T
        far_ref[n, 2] = high
        far_ref[n, 3] = low
        acc_ref[:, rows] += product(vec_oth_ref[:, rows], high, low)
    for q in range(parts):
        at = slice(q * LANES, (q + 1) * LANES)
        here = own_ref[q, 0:cols, :] / own_ref[q, cols + 3 : cols + 4, :]
        image_ref[:, at] = acc_ref[0:cols, at] + acc_ref[cols : 2 * cols, at] + here
    image_ref[:, half:] = acc_ref[0:cols, half:] + acc_ref[cols : 2 * cols, half:]


def second_kernel(core_ref, own_ref, oth_ref, mine_ref, theirs_ref, *refs):
    near, across, far_ref = refs[0:4], refs[4:8], refs[8]
    dir_ref, res_ref, image_ref, send_ref, stat_ref, vec_ref, acc_ref, sum_ref = refs[9:]
    parts, cols = own_ref.shape[0], own_ref.shape[1] - EXTRA
    half = parts * LANES
    panels = half // PANEL
    sum_ref[:, 0:half] = mine_ref[:, 0:half] + theirs_ref[:, half:]
    sum_ref[:, half:] = mine_ref[:, half:] + theirs_ref[:, 0:half]
    blocks = [
        (ref, q, slice(h * half + q * LANES, h * half + (q + 1) * LANES))
        for h, ref in enumerate((own_ref, oth_ref))
        for q in range(parts)
    ]
    zero = jnp.zeros((cols, LANES), F32)
    norm, curve, fresh = zero, zero, zero
    for ref, q, at in blocks:
        value = ref[q, 0:cols, :]
        norm = norm + value * value
        curve = curve + value * sum_ref[:, at]
    norm = jnp.sum(norm, axis=1, keepdims=True)
    step = norm / jnp.sum(curve, axis=1, keepdims=True)
    for ref, q, at in blocks:
        value = ref[q, 0:cols, :] - step * sum_ref[:, at]
        fresh = fresh + value * value
    fresh = jnp.sum(fresh, axis=1, keepdims=True)
    ratio = fresh / norm
    for n, (ref, q, at) in enumerate(blocks):
        value = ref[q, 0:cols, :]
        left = value - step * sum_ref[:, at]
        direction = left + ratio * value
        if n < parts:
            res_ref[:, at] = left
        dir_ref[:, at] = direction
        high, low = split(direction)
        vec_ref[0:cols, at] = high
        vec_ref[cols : 2 * cols, at] = low
    acc_ref[...] = jnp.zeros_like(acc_ref)
    for t, columns, start in near_spans(panels):
        rows, after = slice(t * PANEL, (t + 1) * PANEL), slice((t + 1) * PANEL, half)
        to = slice(start, start + half - rows.start)
        acc_ref[:, columns] += product(vec_ref[:, rows], near[0][:, to], near[1][:, to])
        if after.start < half:
            to = slice(start - rows.start, start - rows.start + half - after.start)
            acc_ref[:, rows] += product(vec_ref[:, after], near[2][to, :], near[3][to, :])
    for t, columns, start in across_spans(panels):
        rows, there = slice(t * PANEL, (t + 1) * PANEL), slice(half, half + columns.stop)
        to = slice(start, start + columns.stop)
        acc_ref[:, there] += product(vec_ref[:, rows], across[0][:, to], across[1][:, to])
        acc_ref[:, rows] += product(vec_ref[:, there], across[2][to, :], across[3][to, :])
    for n in range(panels // 2):
        place = pl.multiple_of((core_ref[0] * (panels // 2) + n) * PANEL, PANEL)
        rows, at = pl.ds(place, PANEL), pl.ds(pl.multiple_of(half + place, PANEL), PANEL)
        acc_ref[:, at] += product(vec_ref[:, rows], far_ref[n, 0], far_ref[n, 1])
        acc_ref[:, rows] += product(vec_ref[:, at], far_ref[n, 2], far_ref[n, 3])
    curve = zero
    for n, (ref, q, at) in enumerate(blocks):
        direction = dir_ref[:, at]
        image = acc_ref[0:cols, at] + acc_ref[cols : 2 * cols, at]
        if n < parts:
            image = image + direction / own_ref[q, cols + 3 : cols + 4, :]
            image_ref[:, at] = image
        else:
            send_ref[:, at.start - half : at.stop - half] = image
        curve = curve + direction * image
    send_ref[:, half:] = curve
    stat_ref[0] = jnp.broadcast_to(step, (cols, LANES))
    stat_ref[1] = jnp.broadcast_to(fresh, (cols, LANES))


def last_kernel(own_ref, dir_ref, res_ref, image_ref, send_ref, come_ref, stat_ref, out_ref):
    parts, cols = own_ref.shape[0], own_ref.shape[1] - EXTRA
    half = parts * LANES
    curve = jnp.sum(send_ref[:, half:] + come_ref[:, half:], axis=1, keepdims=True)
    first = stat_ref[0, :, 0:1]
    step = stat_ref[1, :, 0:1] / curve
    for q in range(parts):
        at = slice(q * LANES, (q + 1) * LANES)
        out_ref[q, 0:cols, :] = first * own_ref[q, 0:cols, :] + step * dir_ref[:, at]
        out_ref[q, cols : 2 * cols, :] = res_ref[:, at] - step * (image_ref[:, at] + come_ref[:, at])


def unpack_kernel(in_ref, sol_ref, res_ref):
    parts, cols = in_ref.shape[0], in_ref.shape[1] // 2
    sol_ref[...] = in_ref[:, 0:cols, :].reshape(parts * cols, LANES).T
    res_ref[...] = in_ref[:, cols : 2 * cols, :].reshape(parts * cols, LANES).T


def shape(*dims, dtype=F32):
    return jax.ShapeDtypeStruct(dims, dtype)


def call(kernel, out, ins, scratch=(), limit=8):
    return pl.pallas_call(
        kernel,
        out_shape=out,
        in_specs=ins,
        out_specs=[VM] * len(out),
        scratch_shapes=list(scratch),
        compiler_params=pltpu.CompilerParams(vmem_limit_bytes=limit << 20),
    )


def by_columns(positions, radii, right_side):
    row_size, col_size = lax.axis_size("row"), lax.axis_size("col")
    devices = row_size * col_size
    parts = devices // 2
    rows, columns = right_side.shape
    total = rows * devices
    cols = columns // parts
    half = total // 2
    panels = half // PANEL
    kernel_scale, softening = constants(total)
    soft = softening / (kernel_scale * kernel_scale)
    groups = [[2 * chip + core for chip in range(parts)] for core in range(2)]
    swap = [(i, i ^ 1) for i in range(col_size)]
    core = (lax.axis_index("col") % 2).astype(jnp.int32).reshape(1)

    (packed,) = call(
        functools.partial(pack_kernel, 1.0 / kernel_scale, parts),
        [shape(parts, cols + EXTRA, LANES)],
        [pl.BlockSpec(memory_space=pltpu.HBM)] * 3,
        [
            pltpu.VMEM((3, LANES), F32),
            pltpu.VMEM((1, LANES), F32),
            pltpu.VMEM((LANES, columns), F32),
            pltpu.SemaphoreType.DMA((3,)),
        ],
        60,
    )(positions, radii.reshape(1, -1), right_side)
    own = lax.all_to_all(packed, AXES, 0, 0, axis_index_groups=groups, tiled=True)
    oth = lax.ppermute(own, "col", swap)
    sizes = [sum(cs.stop - cs.start for _, cs, _ in spans(panels)) for spans in (near_spans, across_spans)]
    *near, vec, sub, acc = call(
        functools.partial(first_kernel, soft),
        [shape(PANEL, sizes[0], dtype=BF16)] * 2
        + [shape(sizes[0] - half, PANEL, dtype=BF16)] * 2
        + [shape(2 * cols, half, dtype=BF16), shape(3, half, LANES), shape(2 * cols, half)],
        [VM],
        [pltpu.VMEM((EXTRA, half), F32)],
        16,
    )(own)
    *across, mine = call(
        functools.partial(middle_kernel, soft),
        [shape(PANEL, sizes[1], dtype=BF16)] * 2
        + [shape(sizes[1], PANEL, dtype=BF16)] * 2
        + [shape(panels // 2, 4, PANEL, PANEL, dtype=BF16), shape(cols, total)],
        [SM] + [VM] * 5,
        [
            pltpu.VMEM((2 * cols, total), F32),
            pltpu.VMEM((EXTRA, half), F32),
            pltpu.VMEM((2 * cols, half), BF16),
        ],
        8,
    )(core, own, oth, vec, sub, acc)
    direction, residual, image, send, stats = call(
        second_kernel,
        [shape(cols, total), shape(cols, half), shape(cols, half), shape(cols, half + LANES), shape(2, cols, LANES)],
        [SM] + [VM] * 13,
        [
            pltpu.VMEM((2 * cols, total), BF16),
            pltpu.VMEM((2 * cols, total), F32),
            pltpu.VMEM((cols, total), F32),
        ],
    )(core, own, oth, mine, lax.ppermute(mine, "col", swap), *near, *across)
    come = lax.ppermute(send, "col", swap)
    (mixed,) = call(last_kernel, [shape(parts, 2 * cols, LANES)], [VM] * 7)(
        own, direction, residual, image, send, come, stats
    )
    mixed = lax.all_to_all(mixed, AXES, 0, 0, axis_index_groups=groups, tiled=True)
    return tuple(call(unpack_kernel, [shape(LANES, columns)] * 2, [VM])(mixed))


def body(positions, radii, right_side):
    devices = lax.axis_size("row") * lax.axis_size("col")
    rows, columns = right_side.shape
    total = rows * devices
    fits = rows == LANES and total % (4 * PANEL) == 0 and 16 * devices == 2 * columns
    if fits and 2 * total * total <= KERNEL_BYTES:
        return by_columns(positions, radii, right_side)
    return blockwise(positions, radii, right_side)


def solution(mesh):
    return jax.shard_map(
        body,
        mesh=mesh,
        in_specs=(P(None, ("row", "col")), P(("row", "col")), P(("row", "col"), None)),
        out_specs=(P(("row", "col"), None), P(("row", "col"), None)),
        check_vma=False,
    )
```

```python
import functools

import jax
import jax.numpy as jnp
from jax import lax
from jax.experimental import pallas as pl
from jax.experimental.pallas import tpu as pltpu
from jax.sharding import PartitionSpec as P

ITERS = 2
AXES = ("row", "col")
F32 = jnp.float32
BF16 = jnp.bfloat16
LANES = 128
EXTRA = 8
PANEL = 256
WIDE = 512
VM = pl.BlockSpec(memory_space=pltpu.VMEM)
SM = pl.BlockSpec(memory_space=pltpu.SMEM)
KERNEL_BYTES = 32 << 20


def constants(total):
    kernel_scale = float(total) ** (-0.5)
    spacing = 0.25 * float(total) ** (-1.0 / 3.0)
    return (kernel_scale, spacing * spacing)


def kernel_product(row_points, col_points, values, kernel_scale, softening, limit):
    row_count = row_points.shape[1]
    col_count = col_points.shape[1]
    blocks = max(1, row_count * col_count // limit)
    while row_count % blocks:
        blocks = blocks - 1
    block_size = row_count // blocks
    grouped = row_points.reshape(3, blocks, block_size).transpose(1, 0, 2)

    def apply_block(row_block):
        first = row_block[0][:, None] - col_points[0][None, :]
        second = row_block[1][:, None] - col_points[1][None, :]
        third = row_block[2][:, None] - col_points[2][None, :]
        squared = first * first + second * second + third * third
        weights = lax.rsqrt(squared + softening) * kernel_scale
        return jnp.dot(
            weights, values, preferred_element_type=jnp.float32, precision=lax.Precision.HIGHEST
        )

    return lax.map(apply_block, grouped).reshape(row_count, values.shape[1])


def squares(residual):
    return lax.psum(jnp.sum(residual * residual, axis=0), AXES)


def blockwise(positions, radii, right_side):
    local_count = positions.shape[1]
    total = local_count * lax.axis_size("row") * lax.axis_size("col")
    kernel_scale, softening = constants(total)
    row_points = lax.all_gather(positions, "col", axis=1, tiled=True)
    col_points = lax.all_gather(positions, "row", axis=1, tiled=True)
    limit = 1 << 20
    solution = jnp.zeros_like(right_side)
    residual = right_side
    direction = right_side
    norm_now = squares(residual)
    for iteration in range(ITERS):
        col_values = lax.all_gather(direction, "row", axis=0, tiled=True)
        summed = lax.psum_scatter(
            kernel_product(row_points, col_points, col_values, kernel_scale, softening, limit),
            "col",
            scatter_dimension=0,
            tiled=True,
        )
        image_vec = direction / radii[:, None] + summed
        curvature = lax.psum(jnp.sum(direction * image_vec, axis=0), AXES)
        step_size = norm_now / curvature
        solution = solution + step_size * direction
        residual = residual - step_size * image_vec
        if iteration + 1 < ITERS:
            norm_next = squares(residual)
            direction = residual + norm_next / norm_now * direction
            norm_now = norm_next
    return (solution, residual)


def pack_kernel(scale, parts, pos_hbm, rad_hbm, rhs_hbm, out_ref, pos_ref, rad_ref, rhs_ref, sems):
    copies = [
        pltpu.make_async_copy(src, dst, sems.at[n])
        for n, (src, dst) in enumerate(((rhs_hbm, rhs_ref), (pos_hbm, pos_ref), (rad_hbm, rad_ref)))
    ]
    for copy in copies:
        copy.start()
    for copy in copies:
        copy.wait()
    cols = rhs_ref.shape[1] // parts
    flipped = rhs_ref[...].T
    extra = jnp.concatenate(
        [pos_ref[...] * scale, rad_ref[...], jnp.zeros((EXTRA - 4, LANES), F32)], axis=0
    )
    for q in range(parts):
        out_ref[q, 0:cols, :] = flipped[q * cols : (q + 1) * cols, :]
        out_ref[q, cols : cols + EXTRA, :] = extra


def split(values):
    high = values.astype(BF16)
    return high, (values - high.astype(F32)).astype(BF16)


def product(vec, high, low):
    cols = vec.shape[0] // 2
    both = jnp.dot(vec, high, preferred_element_type=F32)
    return both[0:cols] + both[cols:] + jnp.dot(vec[0:cols], low, preferred_element_type=F32)


def evaluate(soft, sub_ref, rows, lane_ref, at):
    starts = [sub_ref[c, rows, :] for c in range(3)]
    ends = [lane_ref[c : c + 1, at] for c in range(3)]
    high, low = [], []
    for s in range(0, ends[0].shape[1], LANES):
        gaps = [starts[c] - ends[c][:, s : s + LANES] for c in range(3)]
        squared = gaps[0] * gaps[0] + gaps[1] * gaps[1] + gaps[2] * gaps[2]
        a, b = split(lax.rsqrt(squared + soft))
        high.append(a)
        low.append(b)
    return jnp.concatenate(high, 1), jnp.concatenate(low, 1)


def unpack(ref, lane_ref, vec_ref, sub_ref=None):
    parts, cols = ref.shape[0], ref.shape[1] - EXTRA
    for q in range(parts):
        at = slice(q * LANES, (q + 1) * LANES)
        high, low = split(ref[q, 0:cols, :])
        vec_ref[0:cols, at] = high
        vec_ref[cols : 2 * cols, at] = low
        extra = ref[q, cols : cols + EXTRA, :]
        lane_ref[:, at] = extra
        if sub_ref is not None:
            turned = extra.T
            for c in range(3):
                sub_ref[c, at, :] = jnp.broadcast_to(turned[:, c : c + 1], (LANES, LANES))


def near_spans(panels):
    spans, start = [], 0
    for t in range(panels):
        spans.append((t, slice(t * PANEL, panels * PANEL), start))
        start += (panels - t) * PANEL
    return spans


def across_spans(panels):
    spans, start = [], 0
    for t in range(1, panels):
        spans.append((t, slice(0, t * PANEL), start))
        start += t * PANEL
    return spans


def first_kernel(soft, own_ref, high_ref, low_ref, high_t_ref, low_t_ref, vec_ref, sub_ref, acc_ref, lane_ref):
    panels = vec_ref.shape[1] // PANEL
    unpack(own_ref, lane_ref, vec_ref, sub_ref)
    acc_ref[...] = jnp.zeros_like(acc_ref)
    for t, columns, start in near_spans(panels):
        rows = slice(t * PANEL, (t + 1) * PANEL)
        for c in range(columns.start, columns.stop, WIDE):
            at = slice(c, min(c + WIDE, columns.stop))
            high, low = evaluate(soft, sub_ref, rows, lane_ref, at)
            to = start + c - columns.start
            high_ref[:, to : to + at.stop - c] = high
            low_ref[:, to : to + at.stop - c] = low
            acc_ref[:, at] += product(vec_ref[:, rows], high, low)
            skip = PANEL if c == columns.start else 0
            if at.stop - c > skip:
                high, low = high[:, skip:].T, low[:, skip:].T
                to = to + skip - (t + 1) * PANEL
                high_t_ref[to : to + at.stop - c - skip, :] = high
                low_t_ref[to : to + at.stop - c - skip, :] = low
                acc_ref[:, rows] += product(vec_ref[:, c + skip : at.stop], high, low)


def middle_kernel(soft, core_ref, own_ref, oth_ref, vec_ref, sub_ref, near_ref, *refs):
    high_ref, low_ref, high_t_ref, low_t_ref, far_ref, image_ref, acc_ref, lane_ref, vec_oth_ref = refs
    parts, cols = own_ref.shape[0], own_ref.shape[1] - EXTRA
    half = parts * LANES
    panels = half // PANEL
    unpack(oth_ref, lane_ref, vec_oth_ref)
    acc_ref[:, 0:half] = near_ref[...]
    acc_ref[:, half:] = jnp.zeros_like(near_ref)
    for t, columns, start in across_spans(panels):
        rows = slice(t * PANEL, (t + 1) * PANEL)
        for c in range(columns.start, columns.stop, WIDE):
            at = slice(c, min(c + WIDE, columns.stop))
            high, low = evaluate(soft, sub_ref, rows, lane_ref, at)
            to = slice(start + c, start + at.stop)
            high_ref[:, to] = high
            low_ref[:, to] = low
            acc_ref[:, half + c : half + at.stop] += product(vec_ref[:, rows], high, low)
            high, low = high.T, low.T
            high_t_ref[to, :] = high
            low_t_ref[to, :] = low
            acc_ref[:, rows] += product(vec_oth_ref[:, at], high, low)
    for n in range(panels // 2):
        place = pl.multiple_of((core_ref[0] * (panels // 2) + n) * PANEL, PANEL)
        rows, at = pl.ds(place, PANEL), pl.ds(pl.multiple_of(half + place, PANEL), PANEL)
        high, low = evaluate(soft, sub_ref, rows, lane_ref, rows)
        far_ref[n, 0] = high
        far_ref[n, 1] = low
        acc_ref[:, at] += product(vec_ref[:, rows], high, low)
        high, low = high.T, low.T
        far_ref[n, 2] = high
        far_ref[n, 3] = low
        acc_ref[:, rows] += product(vec_oth_ref[:, rows], high, low)
    for q in range(parts):
        at = slice(q * LANES, (q + 1) * LANES)
        here = own_ref[q, 0:cols, :] / own_ref[q, cols + 3 : cols + 4, :]
        image_ref[:, at] = acc_ref[:, at] + here
    image_ref[:, half:] = acc_ref[:, half:]


def second_kernel(core_ref, own_ref, oth_ref, mine_ref, theirs_ref, *refs):
    near, across, far_ref = refs[0:4], refs[4:8], refs[8]
    dir_ref, res_ref, image_ref, send_ref, stat_ref, vec_ref, acc_ref, sum_ref = refs[9:]
    parts, cols = own_ref.shape[0], own_ref.shape[1] - EXTRA
    half = parts * LANES
    panels = half // PANEL
    sum_ref[:, 0:half] = mine_ref[:, 0:half] + theirs_ref[:, half:]
    sum_ref[:, half:] = mine_ref[:, half:] + theirs_ref[:, 0:half]
    blocks = [
        (ref, q, slice(h * half + q * LANES, h * half + (q + 1) * LANES))
        for h, ref in enumerate((own_ref, oth_ref))
        for q in range(parts)
    ]
    zero = jnp.zeros((cols, LANES), F32)
    norm, curve, fresh = zero, zero, zero
    for ref, q, at in blocks:
        value = ref[q, 0:cols, :]
        norm = norm + value * value
        curve = curve + value * sum_ref[:, at]
    norm = jnp.sum(norm, axis=1, keepdims=True)
    step = norm / jnp.sum(curve, axis=1, keepdims=True)
    for ref, q, at in blocks:
        value = ref[q, 0:cols, :] - step * sum_ref[:, at]
        fresh = fresh + value * value
    fresh = jnp.sum(fresh, axis=1, keepdims=True)
    ratio = fresh / norm
    for n, (ref, q, at) in enumerate(blocks):
        value = ref[q, 0:cols, :]
        left = value - step * sum_ref[:, at]
        direction = left + ratio * value
        if n < parts:
            res_ref[:, at] = left
        dir_ref[:, at] = direction
        high, low = split(direction)
        vec_ref[0:cols, at] = high
        vec_ref[cols : 2 * cols, at] = low
    acc_ref[...] = jnp.zeros_like(acc_ref)
    for t, columns, start in near_spans(panels):
        rows, after = slice(t * PANEL, (t + 1) * PANEL), slice((t + 1) * PANEL, half)
        to = slice(start, start + half - rows.start)
        acc_ref[:, columns] += product(vec_ref[:, rows], near[0][:, to], near[1][:, to])
        if after.start < half:
            to = slice(start - rows.start, start - rows.start + half - after.start)
            acc_ref[:, rows] += product(vec_ref[:, after], near[2][to, :], near[3][to, :])
    for t, columns, start in across_spans(panels):
        rows, there = slice(t * PANEL, (t + 1) * PANEL), slice(half, half + columns.stop)
        to = slice(start, start + columns.stop)
        acc_ref[:, there] += product(vec_ref[:, rows], across[0][:, to], across[1][:, to])
        acc_ref[:, rows] += product(vec_ref[:, there], across[2][to, :], across[3][to, :])
    for n in range(panels // 2):
        place = pl.multiple_of((core_ref[0] * (panels // 2) + n) * PANEL, PANEL)
        rows, at = pl.ds(place, PANEL), pl.ds(pl.multiple_of(half + place, PANEL), PANEL)
        acc_ref[:, at] += product(vec_ref[:, rows], far_ref[n, 0], far_ref[n, 1])
        acc_ref[:, rows] += product(vec_ref[:, at], far_ref[n, 2], far_ref[n, 3])
    curve = zero
    for n, (ref, q, at) in enumerate(blocks):
        direction = dir_ref[:, at]
        image = acc_ref[:, at]
        if n < parts:
            image = image + direction / own_ref[q, cols + 3 : cols + 4, :]
            image_ref[:, at] = image
        else:
            send_ref[:, at.start - half : at.stop - half] = image
        curve = curve + direction * image
    send_ref[:, half:] = curve
    stat_ref[0] = jnp.broadcast_to(step, (cols, LANES))
    stat_ref[1] = jnp.broadcast_to(fresh, (cols, LANES))


def last_kernel(own_ref, dir_ref, res_ref, image_ref, send_ref, come_ref, stat_ref, out_ref):
    parts, cols = own_ref.shape[0], own_ref.shape[1] - EXTRA
    half = parts * LANES
    curve = jnp.sum(send_ref[:, half:] + come_ref[:, half:], axis=1, keepdims=True)
    first = stat_ref[0, :, 0:1]
    step = stat_ref[1, :, 0:1] / curve
    for q in range(parts):
        at = slice(q * LANES, (q + 1) * LANES)
        out_ref[q, 0:cols, :] = first * own_ref[q, 0:cols, :] + step * dir_ref[:, at]
        out_ref[q, cols : 2 * cols, :] = res_ref[:, at] - step * (image_ref[:, at] + come_ref[:, at])


def unpack_kernel(in_ref, sol_ref, res_ref):
    parts, cols = in_ref.shape[0], in_ref.shape[1] // 2
    sol_ref[...] = in_ref[:, 0:cols, :].reshape(parts * cols, LANES).T
    res_ref[...] = in_ref[:, cols : 2 * cols, :].reshape(parts * cols, LANES).T


def shape(*dims, dtype=F32):
    return jax.ShapeDtypeStruct(dims, dtype)


def call(kernel, out, ins, scratch=(), limit=8):
    return pl.pallas_call(
        kernel,
        out_shape=out,
        in_specs=ins,
        out_specs=[VM] * len(out),
        scratch_shapes=list(scratch),
        compiler_params=pltpu.CompilerParams(vmem_limit_bytes=limit << 20),
    )


def by_columns(positions, radii, right_side):
    row_size, col_size = lax.axis_size("row"), lax.axis_size("col")
    devices = row_size * col_size
    parts = devices // 2
    rows, columns = right_side.shape
    total = rows * devices
    cols = columns // parts
    half = total // 2
    panels = half // PANEL
    kernel_scale, softening = constants(total)
    soft = softening / (kernel_scale * kernel_scale)
    groups = [[2 * chip + core for chip in range(parts)] for core in range(2)]
    swap = [(i, i ^ 1) for i in range(col_size)]
    core = (lax.axis_index("col") % 2).astype(jnp.int32).reshape(1)

    (packed,) = call(
        functools.partial(pack_kernel, 1.0 / kernel_scale, parts),
        [shape(parts, cols + EXTRA, LANES)],
        [pl.BlockSpec(memory_space=pltpu.HBM)] * 3,
        [
            pltpu.VMEM((3, LANES), F32),
            pltpu.VMEM((1, LANES), F32),
            pltpu.VMEM((LANES, columns), F32),
            pltpu.SemaphoreType.DMA((3,)),
        ],
    )(*[pltpu.with_memory_space_constraint(x, pltpu.HBM) for x in (positions, radii.reshape(1, -1), right_side)])
    own = lax.all_to_all(packed, AXES, 0, 0, axis_index_groups=groups, tiled=True)
    oth = lax.ppermute(own, "col", swap)
    sizes = [sum(cs.stop - cs.start for _, cs, _ in spans(panels)) for spans in (near_spans, across_spans)]
    *near, vec, sub, acc = call(
        functools.partial(first_kernel, soft),
        [shape(PANEL, sizes[0], dtype=BF16)] * 2
        + [shape(sizes[0] - half, PANEL, dtype=BF16)] * 2
        + [shape(2 * cols, half, dtype=BF16), shape(3, half, LANES), shape(cols, half)],
        [VM],
        [pltpu.VMEM((EXTRA, half), F32)],
        16,
    )(own)
    *across, mine = call(
        functools.partial(middle_kernel, soft),
        [shape(PANEL, sizes[1], dtype=BF16)] * 2
        + [shape(sizes[1], PANEL, dtype=BF16)] * 2
        + [shape(panels // 2, 4, PANEL, PANEL, dtype=BF16), shape(cols, total)],
        [SM] + [VM] * 5,
        [
            pltpu.VMEM((cols, total), F32),
            pltpu.VMEM((EXTRA, half), F32),
            pltpu.VMEM((2 * cols, half), BF16),
        ],
        8,
    )(core, own, oth, vec, sub, acc)
    direction, residual, image, send, stats = call(
        second_kernel,
        [shape(cols, total), shape(cols, half), shape(cols, half), shape(cols, half + LANES), shape(2, cols, LANES)],
        [SM] + [VM] * 13,
        [
            pltpu.VMEM((2 * cols, total), BF16),
            pltpu.VMEM((cols, total), F32),
            pltpu.VMEM((cols, total), F32),
        ],
    )(core, own, oth, mine, lax.ppermute(mine, "col", swap), *near, *across)
    come = lax.ppermute(send, "col", swap)
    (mixed,) = call(last_kernel, [shape(parts, 2 * cols, LANES)], [VM] * 7)(
        own, direction, residual, image, send, come, stats
    )
    mixed = lax.all_to_all(mixed, AXES, 0, 0, axis_index_groups=groups, tiled=True)
    return tuple(call(unpack_kernel, [shape(LANES, columns)] * 2, [VM])(mixed))


def body(positions, radii, right_side):
    devices = lax.axis_size("row") * lax.axis_size("col")
    rows, columns = right_side.shape
    total = rows * devices
    fits = rows == LANES and total % (4 * PANEL) == 0 and 16 * devices == 2 * columns
    if fits and 2 * total * total <= KERNEL_BYTES:
        return by_columns(positions, radii, right_side)
    return blockwise(positions, radii, right_side)


def solution(mesh):
    return jax.shard_map(
        body,
        mesh=mesh,
        in_specs=(P(None, ("row", "col")), P(("row", "col")), P(("row", "col"), None)),
        out_specs=(P(("row", "col"), None), P(("row", "col"), None)),
        check_vma=False,
    )
```

```python
import functools

import jax
import jax.numpy as jnp
from jax import lax
from jax.experimental import pallas as pl
from jax.experimental.pallas import tpu as pltpu
from jax.sharding import PartitionSpec as P

ITERS = 2
AXES = ("row", "col")
F32 = jnp.float32
BF16 = jnp.bfloat16
LANES = 128
EXTRA = 8
PANEL = 256
WIDE = 1024
AHEAD = 2
DEPTH = 48
VM = pl.BlockSpec(memory_space=pltpu.VMEM)
SM = pl.BlockSpec(memory_space=pltpu.SMEM)
KERNEL_BYTES = 32 << 20


def constants(total):
    kernel_scale = float(total) ** (-0.5)
    spacing = 0.25 * float(total) ** (-1.0 / 3.0)
    return (kernel_scale, spacing * spacing)


def kernel_product(row_points, col_points, values, kernel_scale, softening, limit):
    row_count = row_points.shape[1]
    col_count = col_points.shape[1]
    blocks = max(1, row_count * col_count // limit)
    while row_count % blocks:
        blocks = blocks - 1
    block_size = row_count // blocks
    grouped = row_points.reshape(3, blocks, block_size).transpose(1, 0, 2)

    def apply_block(row_block):
        first = row_block[0][:, None] - col_points[0][None, :]
        second = row_block[1][:, None] - col_points[1][None, :]
        third = row_block[2][:, None] - col_points[2][None, :]
        squared = first * first + second * second + third * third
        weights = lax.rsqrt(squared + softening) * kernel_scale
        return jnp.dot(
            weights, values, preferred_element_type=jnp.float32, precision=lax.Precision.HIGHEST
        )

    return lax.map(apply_block, grouped).reshape(row_count, values.shape[1])


def squares(residual):
    return lax.psum(jnp.sum(residual * residual, axis=0), AXES)


def blockwise(positions, radii, right_side):
    local_count = positions.shape[1]
    total = local_count * lax.axis_size("row") * lax.axis_size("col")
    kernel_scale, softening = constants(total)
    row_points = lax.all_gather(positions, "col", axis=1, tiled=True)
    col_points = lax.all_gather(positions, "row", axis=1, tiled=True)
    limit = 1 << 20
    solution = jnp.zeros_like(right_side)
    residual = right_side
    direction = right_side
    norm_now = squares(residual)
    for iteration in range(ITERS):
        col_values = lax.all_gather(direction, "row", axis=0, tiled=True)
        summed = lax.psum_scatter(
            kernel_product(row_points, col_points, col_values, kernel_scale, softening, limit),
            "col",
            scatter_dimension=0,
            tiled=True,
        )
        image_vec = direction / radii[:, None] + summed
        curvature = lax.psum(jnp.sum(direction * image_vec, axis=0), AXES)
        step_size = norm_now / curvature
        solution = solution + step_size * direction
        residual = residual - step_size * image_vec
        if iteration + 1 < ITERS:
            norm_next = squares(residual)
            direction = residual + norm_next / norm_now * direction
            norm_now = norm_next
    return (solution, residual)


def pack_kernel(parts, pos_hbm, rad_hbm, rhs_hbm, out_ref, pos_ref, rad_ref, rhs_ref, sems):
    copies = [
        pltpu.make_async_copy(src, dst, sems.at[n])
        for n, (src, dst) in enumerate(((rhs_hbm, rhs_ref), (pos_hbm, pos_ref), (rad_hbm, rad_ref)))
    ]
    for copy in copies:
        copy.start()
    for copy in copies:
        copy.wait()
    cols = rhs_ref.shape[1] // parts
    flipped = rhs_ref[...].T
    extra = jnp.concatenate(
        [pos_ref[...], rad_ref[...], jnp.zeros((EXTRA - 4, LANES), F32)], axis=0
    )
    for q in range(parts):
        out_ref[q, 0:cols, :] = flipped[q * cols : (q + 1) * cols, :]
        out_ref[q, cols : cols + EXTRA, :] = extra


def split(values):
    high = values.astype(BF16)
    return high, (values - high.astype(F32)).astype(BF16)


def product(vec, high, low):
    cols = vec.shape[0] // 2
    both = jnp.dot(vec, high, preferred_element_type=F32)
    return both[0:cols] + both[cols:] + jnp.dot(vec[0:cols], low, preferred_element_type=F32)


def evaluate(left_ref, right_ref, tasks):
    begun = []
    for n in range(len(tasks) + AHEAD):
        if n < len(tasks):
            rows, at, _ = tasks[n]
            begun.append(jnp.dot(left_ref[rows, :], right_ref[:, at], preferred_element_type=F32))
        if n >= AHEAD:
            tasks[n - AHEAD][2](*split(lax.rsqrt(begun[n - AHEAD])))


def pieces(values, count):
    out = []
    for _ in range(count):
        part = values.astype(BF16).astype(F32)
        values = values - part
        out.append(part)
    return out


def factors(ref, soft, fact_ref, right_ref, left_ref=None):
    parts, cols = ref.shape[0], ref.shape[1] - EXTRA
    place = jnp.concatenate([ref[q, cols : cols + 3, :] for q in range(parts)], axis=1) * 512.0 - 256.0
    whole = jnp.floor(place + 0.5)
    rest, more = pieces(place - whole, 2)
    both = rest + more
    one = jnp.ones_like(place[0:1])
    norm = pieces(jnp.sum(whole * whole, axis=0, keepdims=True), 3)
    cross = jnp.sum((2.0 * whole + both) * both, axis=0, keepdims=True)

    def write(rows):
        at = 0
        for row in rows:
            fact_ref[at : at + row.shape[0], :] = row
            at += row.shape[0]

    fact_ref[...] = jnp.zeros_like(fact_ref)
    twice, less, least = -2.0 * whole, -2.0 * rest, -2.0 * more
    write([twice, one, one, one, *norm, one, one, one, *pieces(cross + soft, 3), less, least, twice, twice, less, least, less])
    right_ref[...] = fact_ref[0 : right_ref.shape[0], :].astype(BF16)
    if left_ref is not None:
        write([whole, *norm, one, one, one, *pieces(cross, 3), one, one, one, whole, whole, rest, more, rest, rest, more])
        for q in range(parts):
            at = slice(q * LANES, (q + 1) * LANES)
            left_ref[at, :] = fact_ref[:, at].T[:, 0 : left_ref.shape[1]].astype(BF16)


def unpack(factor, ref, vec_ref):
    parts, cols = ref.shape[0], ref.shape[1] - EXTRA
    for q in range(parts):
        at = slice(q * LANES, (q + 1) * LANES)
        high, low = split(ref[q, 0:cols, :] * factor)
        vec_ref[0:cols, at] = high
        vec_ref[cols : 2 * cols, at] = low


def near_spans(panels):
    spans, start = [], 0
    for t in range(panels):
        spans.append((t, slice(t * PANEL, panels * PANEL), start))
        start += (panels - t) * PANEL
    return spans


def across_spans(panels):
    spans, start = [], 0
    for t in range(1, panels):
        spans.append((t, slice(0, t * PANEL), start))
        start += t * PANEL
    return spans


def first_kernel(soft, factor, own_ref, high_ref, low_ref, high_t_ref, low_t_ref, vec_ref, left_ref, acc_ref, right_ref, fact_ref):
    panels = vec_ref.shape[1] // PANEL
    unpack(factor, own_ref, vec_ref)
    factors(own_ref, soft, fact_ref, right_ref, left_ref)
    acc_ref[...] = jnp.zeros_like(acc_ref)
    tasks = []
    for t, columns, start in near_spans(panels):
        rows = slice(t * PANEL, (t + 1) * PANEL)
        for c in range(columns.start, columns.stop, WIDE):
            at = slice(c, min(c + WIDE, columns.stop))

            def use(high, low, t=t, rows=rows, at=at, to=start + c - columns.start, skip=PANEL if c == columns.start else 0):
                wide = at.stop - at.start
                high_ref[:, to : to + wide] = high
                low_ref[:, to : to + wide] = low
                acc_ref[:, at] += product(vec_ref[:, rows], high, low)
                if wide > skip:
                    high, low = high[:, skip:].T, low[:, skip:].T
                    to = to + skip - (t + 1) * PANEL
                    high_t_ref[to : to + wide - skip, :] = high
                    low_t_ref[to : to + wide - skip, :] = low
                    acc_ref[:, rows] += product(vec_ref[:, at.start + skip : at.stop], high, low)

            tasks.append((rows, at, use))
    evaluate(left_ref, right_ref, tasks)


def middle_kernel(soft, factor, core_ref, own_ref, oth_ref, vec_ref, left_ref, near_ref, *refs):
    high_ref, low_ref, high_t_ref, low_t_ref, far_ref, image_ref, acc_ref, right_ref, vec_oth_ref, fact_ref = refs
    parts, cols = own_ref.shape[0], own_ref.shape[1] - EXTRA
    half = parts * LANES
    panels = half // PANEL
    unpack(factor, oth_ref, vec_oth_ref)
    factors(oth_ref, soft, fact_ref, right_ref)
    acc_ref[:, 0:half] = near_ref[...]
    acc_ref[:, half:] = jnp.zeros_like(near_ref)
    tasks = []
    for n in range(panels // 2):
        place = pl.multiple_of((core_ref[0] * (panels // 2) + n) * PANEL, PANEL)
        rows, there = pl.ds(place, PANEL), pl.ds(pl.multiple_of(half + place, PANEL), PANEL)

        def use_far(high, low, n=n, rows=rows, there=there):
            far_ref[n, 0] = high
            far_ref[n, 1] = low
            acc_ref[:, there] += product(vec_ref[:, rows], high, low)
            high, low = high.T, low.T
            far_ref[n, 2] = high
            far_ref[n, 3] = low
            acc_ref[:, rows] += product(vec_oth_ref[:, rows], high, low)

        tasks.append((rows, rows, use_far))
    for t, columns, start in across_spans(panels):
        rows = slice(t * PANEL, (t + 1) * PANEL)
        for c in range(columns.start, columns.stop, WIDE):
            at = slice(c, min(c + WIDE, columns.stop))

            def use(high, low, rows=rows, at=at, to=slice(start + c, start + at.stop)):
                high_ref[:, to] = high
                low_ref[:, to] = low
                acc_ref[:, half + at.start : half + at.stop] += product(vec_ref[:, rows], high, low)
                high, low = high.T, low.T
                high_t_ref[to, :] = high
                low_t_ref[to, :] = low
                acc_ref[:, rows] += product(vec_oth_ref[:, at], high, low)

            tasks.append((rows, at, use))
    evaluate(left_ref, right_ref, tasks)
    for q in range(parts):
        at = slice(q * LANES, (q + 1) * LANES)
        here = own_ref[q, 0:cols, :] / own_ref[q, cols + 3 : cols + 4, :]
        image_ref[:, at] = acc_ref[:, at] + here
    image_ref[:, half:] = acc_ref[:, half:]


def second_kernel(factor, core_ref, own_ref, oth_ref, mine_ref, theirs_ref, *refs):
    near, across, far_ref = refs[0:4], refs[4:8], refs[8]
    dir_ref, res_ref, image_ref, send_ref, stat_ref, vec_ref, acc_ref, sum_ref = refs[9:]
    parts, cols = own_ref.shape[0], own_ref.shape[1] - EXTRA
    half = parts * LANES
    panels = half // PANEL
    sum_ref[:, 0:half] = mine_ref[:, 0:half] + theirs_ref[:, half:]
    sum_ref[:, half:] = mine_ref[:, half:] + theirs_ref[:, 0:half]
    blocks = [
        (ref, q, slice(h * half + q * LANES, h * half + (q + 1) * LANES))
        for h, ref in enumerate((own_ref, oth_ref))
        for q in range(parts)
    ]
    zero = jnp.zeros((cols, LANES), F32)
    norm, curve, fresh = zero, zero, zero
    for ref, q, at in blocks:
        value = ref[q, 0:cols, :]
        norm = norm + value * value
        curve = curve + value * sum_ref[:, at]
    norm = jnp.sum(norm, axis=1, keepdims=True)
    step = norm / jnp.sum(curve, axis=1, keepdims=True)
    for ref, q, at in blocks:
        value = ref[q, 0:cols, :] - step * sum_ref[:, at]
        fresh = fresh + value * value
    fresh = jnp.sum(fresh, axis=1, keepdims=True)
    ratio = fresh / norm
    for n, (ref, q, at) in enumerate(blocks):
        value = ref[q, 0:cols, :]
        left = value - step * sum_ref[:, at]
        direction = left + ratio * value
        if n < parts:
            res_ref[:, at] = left
        dir_ref[:, at] = direction
        high, low = split(direction * factor)
        vec_ref[0:cols, at] = high
        vec_ref[cols : 2 * cols, at] = low
    acc_ref[...] = jnp.zeros_like(acc_ref)
    for t, columns, start in near_spans(panels):
        rows, after = slice(t * PANEL, (t + 1) * PANEL), slice((t + 1) * PANEL, half)
        to = slice(start, start + half - rows.start)
        acc_ref[:, columns] += product(vec_ref[:, rows], near[0][:, to], near[1][:, to])
        if after.start < half:
            to = slice(start - rows.start, start - rows.start + half - after.start)
            acc_ref[:, rows] += product(vec_ref[:, after], near[2][to, :], near[3][to, :])
    for t, columns, start in across_spans(panels):
        rows, there = slice(t * PANEL, (t + 1) * PANEL), slice(half, half + columns.stop)
        to = slice(start, start + columns.stop)
        acc_ref[:, there] += product(vec_ref[:, rows], across[0][:, to], across[1][:, to])
        acc_ref[:, rows] += product(vec_ref[:, there], across[2][to, :], across[3][to, :])
    for n in range(panels // 2):
        place = pl.multiple_of((core_ref[0] * (panels // 2) + n) * PANEL, PANEL)
        rows, at = pl.ds(place, PANEL), pl.ds(pl.multiple_of(half + place, PANEL), PANEL)
        acc_ref[:, at] += product(vec_ref[:, rows], far_ref[n, 0], far_ref[n, 1])
        acc_ref[:, rows] += product(vec_ref[:, at], far_ref[n, 2], far_ref[n, 3])
    curve = zero
    for n, (ref, q, at) in enumerate(blocks):
        direction = dir_ref[:, at]
        image = acc_ref[:, at]
        if n < parts:
            image = image + direction / own_ref[q, cols + 3 : cols + 4, :]
            image_ref[:, at] = image
        else:
            send_ref[:, at.start - half : at.stop - half] = image
        curve = curve + direction * image
    send_ref[:, half:] = curve
    stat_ref[0] = jnp.broadcast_to(step, (cols, LANES))
    stat_ref[1] = jnp.broadcast_to(fresh, (cols, LANES))


def last_kernel(own_ref, dir_ref, res_ref, image_ref, send_ref, come_ref, stat_ref, out_ref):
    parts, cols = own_ref.shape[0], own_ref.shape[1] - EXTRA
    half = parts * LANES
    curve = jnp.sum(send_ref[:, half:] + come_ref[:, half:], axis=1, keepdims=True)
    first = stat_ref[0, :, 0:1]
    step = stat_ref[1, :, 0:1] / curve
    for q in range(parts):
        at = slice(q * LANES, (q + 1) * LANES)
        out_ref[q, 0:cols, :] = first * own_ref[q, 0:cols, :] + step * dir_ref[:, at]
        out_ref[q, cols : 2 * cols, :] = res_ref[:, at] - step * (image_ref[:, at] + come_ref[:, at])


def unpack_kernel(in_ref, sol_ref, res_ref):
    parts, cols = in_ref.shape[0], in_ref.shape[1] // 2
    sol_ref[...] = in_ref[:, 0:cols, :].reshape(parts * cols, LANES).T
    res_ref[...] = in_ref[:, cols : 2 * cols, :].reshape(parts * cols, LANES).T


def shape(*dims, dtype=F32):
    return jax.ShapeDtypeStruct(dims, dtype)


def call(kernel, out, ins, scratch=(), limit=8):
    return pl.pallas_call(
        kernel,
        out_shape=out,
        in_specs=ins,
        out_specs=[VM] * len(out),
        scratch_shapes=list(scratch),
        compiler_params=pltpu.CompilerParams(vmem_limit_bytes=limit << 20),
    )


def by_columns(positions, radii, right_side):
    row_size, col_size = lax.axis_size("row"), lax.axis_size("col")
    devices = row_size * col_size
    parts = devices // 2
    rows, columns = right_side.shape
    total = rows * devices
    cols = columns // parts
    half = total // 2
    panels = half // PANEL
    kernel_scale, softening = constants(total)
    soft, factor = softening * 4.0**9, kernel_scale * 2.0**9
    groups = [[2 * chip + core for chip in range(parts)] for core in range(2)]
    swap = [(i, i ^ 1) for i in range(col_size)]
    core = (lax.axis_index("col") % 2).astype(jnp.int32).reshape(1)

    (packed,) = call(
        functools.partial(pack_kernel, parts),
        [shape(parts, cols + EXTRA, LANES)],
        [pl.BlockSpec(memory_space=pltpu.HBM)] * 3,
        [
            pltpu.VMEM((3, LANES), F32),
            pltpu.VMEM((1, LANES), F32),
            pltpu.VMEM((LANES, columns), F32),
            pltpu.SemaphoreType.DMA((3,)),
        ],
    )(*[pltpu.with_memory_space_constraint(x, pltpu.HBM) for x in (positions, radii.reshape(1, -1), right_side)])
    own = lax.all_to_all(packed, AXES, 0, 0, axis_index_groups=groups, tiled=True)
    oth = lax.ppermute(own, "col", swap)
    sizes = [sum(cs.stop - cs.start for _, cs, _ in spans(panels)) for spans in (near_spans, across_spans)]
    *near, vec, left, acc = call(
        functools.partial(first_kernel, soft, factor),
        [shape(PANEL, sizes[0], dtype=BF16)] * 2
        + [shape(sizes[0] - half, PANEL, dtype=BF16)] * 2
        + [shape(2 * cols, half, dtype=BF16), shape(half, DEPTH, dtype=BF16), shape(cols, half)],
        [VM],
        [pltpu.VMEM((DEPTH, half), BF16), pltpu.VMEM((LANES, half), F32)],
        16,
    )(own)
    *across, mine = call(
        functools.partial(middle_kernel, soft, factor),
        [shape(PANEL, sizes[1], dtype=BF16)] * 2
        + [shape(sizes[1], PANEL, dtype=BF16)] * 2
        + [shape(panels // 2, 4, PANEL, PANEL, dtype=BF16), shape(cols, total)],
        [SM] + [VM] * 5,
        [
            pltpu.VMEM((cols, total), F32),
            pltpu.VMEM((DEPTH, half), BF16),
            pltpu.VMEM((2 * cols, half), BF16),
            pltpu.VMEM((LANES, half), F32),
        ],
        8,
    )(core, own, oth, vec, left, acc)
    direction, residual, image, send, stats = call(
        functools.partial(second_kernel, factor),
        [shape(cols, total), shape(cols, half), shape(cols, half), shape(cols, half + LANES), shape(2, cols, LANES)],
        [SM] + [VM] * 13,
        [
            pltpu.VMEM((2 * cols, total), BF16),
            pltpu.VMEM((cols, total), F32),
            pltpu.VMEM((cols, total), F32),
        ],
    )(core, own, oth, mine, lax.ppermute(mine, "col", swap), *near, *across)
    come = lax.ppermute(send, "col", swap)
    (mixed,) = call(last_kernel, [shape(parts, 2 * cols, LANES)], [VM] * 7)(
        own, direction, residual, image, send, come, stats
    )
    mixed = lax.all_to_all(mixed, AXES, 0, 0, axis_index_groups=groups, tiled=True)
    return tuple(call(unpack_kernel, [shape(LANES, columns)] * 2, [VM])(mixed))


def body(positions, radii, right_side):
    devices = lax.axis_size("row") * lax.axis_size("col")
    rows, columns = right_side.shape
    total = rows * devices
    fits = rows == LANES and total % (4 * PANEL) == 0 and 16 * devices == 2 * columns
    if fits and 2 * total * total <= KERNEL_BYTES:
        return by_columns(positions, radii, right_side)
    return blockwise(positions, radii, right_side)


def solution(mesh):
    return jax.shard_map(
        body,
        mesh=mesh,
        in_specs=(P(None, ("row", "col")), P(("row", "col")), P(("row", "col"), None)),
        out_specs=(P(("row", "col"), None), P(("row", "col"), None)),
        check_vma=False,
    )
```

```python
import functools

import jax
import jax.numpy as jnp
from jax import lax
from jax.experimental import pallas as pl
from jax.experimental.pallas import tpu as pltpu
from jax.sharding import PartitionSpec as P

ITERS = 2
AXES = ("row", "col")
F32 = jnp.float32
BF16 = jnp.bfloat16
LANES = 128
EXTRA = 4
PANEL = 256
WIDE = 1024
AHEAD = 2
COPIES = 4
DEPTH = 48
VM = pl.BlockSpec(memory_space=pltpu.VMEM)
SM = pl.BlockSpec(memory_space=pltpu.SMEM)
KERNEL_BYTES = 32 << 20


def constants(total):
    kernel_scale = float(total) ** (-0.5)
    spacing = 0.25 * float(total) ** (-1.0 / 3.0)
    return (kernel_scale, spacing * spacing)


def kernel_product(row_points, col_points, values, kernel_scale, softening, limit):
    row_count = row_points.shape[1]
    col_count = col_points.shape[1]
    blocks = max(1, row_count * col_count // limit)
    while row_count % blocks:
        blocks = blocks - 1
    block_size = row_count // blocks
    grouped = row_points.reshape(3, blocks, block_size).transpose(1, 0, 2)

    def apply_block(row_block):
        first = row_block[0][:, None] - col_points[0][None, :]
        second = row_block[1][:, None] - col_points[1][None, :]
        third = row_block[2][:, None] - col_points[2][None, :]
        squared = first * first + second * second + third * third
        weights = lax.rsqrt(squared + softening) * kernel_scale
        return jnp.dot(
            weights, values, preferred_element_type=jnp.float32, precision=lax.Precision.HIGHEST
        )

    return lax.map(apply_block, grouped).reshape(row_count, values.shape[1])


def squares(residual):
    return lax.psum(jnp.sum(residual * residual, axis=0), AXES)


def blockwise(positions, radii, right_side):
    local_count = positions.shape[1]
    total = local_count * lax.axis_size("row") * lax.axis_size("col")
    kernel_scale, softening = constants(total)
    row_points = lax.all_gather(positions, "col", axis=1, tiled=True)
    col_points = lax.all_gather(positions, "row", axis=1, tiled=True)
    limit = 1 << 20
    solution = jnp.zeros_like(right_side)
    residual = right_side
    direction = right_side
    norm_now = squares(residual)
    for iteration in range(ITERS):
        col_values = lax.all_gather(direction, "row", axis=0, tiled=True)
        summed = lax.psum_scatter(
            kernel_product(row_points, col_points, col_values, kernel_scale, softening, limit),
            "col",
            scatter_dimension=0,
            tiled=True,
        )
        image_vec = direction / radii[:, None] + summed
        curvature = lax.psum(jnp.sum(direction * image_vec, axis=0), AXES)
        step_size = norm_now / curvature
        solution = solution + step_size * direction
        residual = residual - step_size * image_vec
        if iteration + 1 < ITERS:
            norm_next = squares(residual)
            direction = residual + norm_next / norm_now * direction
            norm_now = norm_next
    return (solution, residual)


def pack_kernel(parts, pos_hbm, rad_hbm, rhs_hbm, out_ref, pos_ref, rad_ref, rhs_ref, sems):
    rows = [pl.ds(n * (LANES // COPIES), LANES // COPIES) for n in range(COPIES)]
    ends = [(rhs_hbm.at[at], rhs_ref.at[at]) for at in rows] + [(pos_hbm, pos_ref), (rad_hbm, rad_ref)]
    copies = [pltpu.make_async_copy(src, dst, sems.at[n]) for n, (src, dst) in enumerate(ends)]
    for copy in copies:
        copy.start()
    for copy in copies:
        copy.wait()
    cols = rhs_ref.shape[1] // parts
    flipped = rhs_ref[...].T
    extra = jnp.concatenate([pos_ref[...], rad_ref[...]], axis=0)
    for q in range(parts):
        for n in range(cols // EXTRA):
            out_ref[q, n] = flipped[q * cols + n * EXTRA : q * cols + (n + 1) * EXTRA, :]
        out_ref[q, cols // EXTRA] = extra


def split(values):
    high = values.astype(BF16)
    return high, (values - high.astype(F32)).astype(BF16)


def product(vec, high, low):
    cols = vec.shape[0] // 2
    both = jnp.dot(vec, high, preferred_element_type=F32)
    return both[0:cols] + both[cols:] + jnp.dot(vec[0:cols], low, preferred_element_type=F32)


def evaluate(left_ref, right_ref, tasks):
    begun = []
    for n in range(len(tasks) + AHEAD):
        if n < len(tasks):
            rows, at, _ = tasks[n]
            begun.append(jnp.dot(left_ref[rows, :], right_ref[:, at], preferred_element_type=F32))
        if n >= AHEAD:
            tasks[n - AHEAD][2](*split(lax.rsqrt(begun[n - AHEAD])))


def pieces(values, count):
    out = []
    for _ in range(count):
        part = values.astype(BF16).astype(F32)
        values = values - part
        out.append(part)
    return out


def factors(flat_ref, soft, fact_ref, right_ref, left_ref=None):
    cols = flat_ref.shape[0] - EXTRA
    place = flat_ref[cols : cols + 3, :] * 512.0 - 256.0
    whole = jnp.floor(place + 0.5)
    rest, more = pieces(place - whole, 2)
    both = rest + more
    one = jnp.ones_like(place[0:1])
    norm = pieces(jnp.sum(whole * whole, axis=0, keepdims=True), 3)
    cross = jnp.sum((2.0 * whole + both) * both, axis=0, keepdims=True)

    def write(rows):
        at = 0
        for row in rows:
            fact_ref[at : at + row.shape[0], :] = row
            at += row.shape[0]

    fact_ref[32:, :] = jnp.zeros_like(fact_ref[32:, :])
    twice, less, least = -2.0 * whole, -2.0 * rest, -2.0 * more
    write([twice, one, one, one, *norm, one, one, one, *pieces(cross + soft, 3), less, least, twice, twice, less, least, less])
    right_ref[...] = fact_ref[...].astype(BF16)
    if left_ref is not None:
        write([whole, *norm, one, one, one, *pieces(cross, 3), one, one, one, whole, whole, rest, more, rest, rest, more])
        for q in range(flat_ref.shape[1] // LANES):
            at = slice(q * LANES, (q + 1) * LANES)
            left_ref[at, :] = fact_ref[:, at].T.astype(BF16)


def unpack(factor, ref, flat_ref, vec_ref):
    cols = flat_ref.shape[0] - EXTRA
    for q in range(ref.shape[0]):
        at = slice(q * LANES, (q + 1) * LANES)
        flat_ref[:, at] = jnp.concatenate([ref[q, n] for n in range(ref.shape[1])], axis=0)
        high, low = split(flat_ref[0:cols, at] * factor)
        vec_ref[0:cols, at] = high
        vec_ref[cols : 2 * cols, at] = low


def near_spans(panels):
    spans, start = [], 0
    for t in range(panels):
        spans.append((t, slice(t * PANEL, panels * PANEL), start))
        start += (panels - t) * PANEL
    return spans


def across_spans(panels):
    spans, start = [], 0
    for t in range(1, panels):
        spans.append((t, slice(0, t * PANEL), start))
        start += t * PANEL
    return spans


def first_kernel(soft, factor, own_ref, high_ref, low_ref, high_t_ref, low_t_ref, vec_ref, left_ref, acc_ref, flat_ref, right_ref, fact_ref):
    panels = vec_ref.shape[1] // PANEL
    unpack(factor, own_ref, flat_ref, vec_ref)
    factors(flat_ref, soft, fact_ref, right_ref, left_ref)
    acc_ref[...] = jnp.zeros_like(acc_ref)
    tasks = []
    for t, columns, start in near_spans(panels):
        rows = slice(t * PANEL, (t + 1) * PANEL)
        for c in range(columns.start, columns.stop, WIDE):
            at = slice(c, min(c + WIDE, columns.stop))

            def use(high, low, t=t, rows=rows, at=at, to=start + c - columns.start, skip=PANEL if c == columns.start else 0):
                wide = at.stop - at.start
                high_ref[:, to : to + wide] = high
                low_ref[:, to : to + wide] = low
                acc_ref[:, at] += product(vec_ref[:, rows], high, low)
                if wide > skip:
                    high, low = high[:, skip:].T, low[:, skip:].T
                    to = to + skip - (t + 1) * PANEL
                    high_t_ref[to : to + wide - skip, :] = high
                    low_t_ref[to : to + wide - skip, :] = low
                    acc_ref[:, rows] += product(vec_ref[:, at.start + skip : at.stop], high, low)

            tasks.append((rows, at, use))
    evaluate(left_ref, right_ref, tasks)


def middle_kernel(soft, factor, core_ref, own_ref, oth_ref, vec_ref, left_ref, near_ref, *refs):
    high_ref, low_ref, high_t_ref, low_t_ref, far_ref, image_ref, flat_ref, acc_ref, right_ref, vec_oth_ref, fact_ref = refs
    cols, half = own_ref.shape[0] - EXTRA, own_ref.shape[1]
    parts = half // LANES
    panels = half // PANEL
    unpack(factor, oth_ref, flat_ref, vec_oth_ref)
    factors(flat_ref, soft, fact_ref, right_ref)
    acc_ref[:, 0:half] = near_ref[...]
    acc_ref[:, half:] = jnp.zeros_like(near_ref)
    tasks = []
    for n in range(panels // 2):
        place = pl.multiple_of((core_ref[0] * (panels // 2) + n) * PANEL, PANEL)
        rows, there = pl.ds(place, PANEL), pl.ds(pl.multiple_of(half + place, PANEL), PANEL)

        def use_far(high, low, n=n, rows=rows, there=there):
            far_ref[n, 0] = high
            far_ref[n, 1] = low
            acc_ref[:, there] += product(vec_ref[:, rows], high, low)
            high, low = high.T, low.T
            far_ref[n, 2] = high
            far_ref[n, 3] = low
            acc_ref[:, rows] += product(vec_oth_ref[:, rows], high, low)

        tasks.append((rows, rows, use_far))
    for t, columns, start in across_spans(panels):
        rows = slice(t * PANEL, (t + 1) * PANEL)
        for c in range(columns.start, columns.stop, WIDE):
            at = slice(c, min(c + WIDE, columns.stop))

            def use(high, low, rows=rows, at=at, to=slice(start + c, start + at.stop)):
                high_ref[:, to] = high
                low_ref[:, to] = low
                acc_ref[:, half + at.start : half + at.stop] += product(vec_ref[:, rows], high, low)
                high, low = high.T, low.T
                high_t_ref[to, :] = high
                low_t_ref[to, :] = low
                acc_ref[:, rows] += product(vec_oth_ref[:, at], high, low)

            tasks.append((rows, at, use))
    evaluate(left_ref, right_ref, tasks)
    for q in range(parts):
        at = slice(q * LANES, (q + 1) * LANES)
        here = own_ref[0:cols, at] / own_ref[cols + 3 : cols + 4, at]
        image_ref[:, at] = acc_ref[:, at] + here
    image_ref[:, half:] = acc_ref[:, half:]


def second_kernel(factor, core_ref, own_ref, oth_ref, mine_ref, theirs_ref, *refs):
    near, across, far_ref = refs[0:4], refs[4:8], refs[8]
    dir_ref, res_ref, image_ref, send_ref, stat_ref, vec_ref, acc_ref, sum_ref = refs[9:]
    cols, half = own_ref.shape[0] - EXTRA, own_ref.shape[1]
    parts = half // LANES
    panels = half // PANEL
    sum_ref[:, 0:half] = mine_ref[:, 0:half] + theirs_ref[:, half:]
    sum_ref[:, half:] = mine_ref[:, half:] + theirs_ref[:, 0:half]
    blocks = [
        (ref, slice(q * LANES, (q + 1) * LANES), slice(h * half + q * LANES, h * half + (q + 1) * LANES))
        for h, ref in enumerate((own_ref, oth_ref))
        for q in range(parts)
    ]
    zero = jnp.zeros((cols, LANES), F32)
    norm, curve, fresh = zero, zero, zero
    for ref, q, at in blocks:
        value = ref[0:cols, q]
        norm = norm + value * value
        curve = curve + value * sum_ref[:, at]
    norm = jnp.sum(norm, axis=1, keepdims=True)
    step = norm / jnp.sum(curve, axis=1, keepdims=True)
    for ref, q, at in blocks:
        value = ref[0:cols, q] - step * sum_ref[:, at]
        fresh = fresh + value * value
    fresh = jnp.sum(fresh, axis=1, keepdims=True)
    ratio = fresh / norm
    for n, (ref, q, at) in enumerate(blocks):
        value = ref[0:cols, q]
        left = value - step * sum_ref[:, at]
        direction = left + ratio * value
        if n < parts:
            res_ref[:, at] = left
        dir_ref[:, at] = direction
        high, low = split(direction * factor)
        vec_ref[0:cols, at] = high
        vec_ref[cols : 2 * cols, at] = low
    acc_ref[...] = jnp.zeros_like(acc_ref)
    for t, columns, start in near_spans(panels):
        rows, after = slice(t * PANEL, (t + 1) * PANEL), slice((t + 1) * PANEL, half)
        to = slice(start, start + half - rows.start)
        acc_ref[:, columns] += product(vec_ref[:, rows], near[0][:, to], near[1][:, to])
        if after.start < half:
            to = slice(start - rows.start, start - rows.start + half - after.start)
            acc_ref[:, rows] += product(vec_ref[:, after], near[2][to, :], near[3][to, :])
    for t, columns, start in across_spans(panels):
        rows, there = slice(t * PANEL, (t + 1) * PANEL), slice(half, half + columns.stop)
        to = slice(start, start + columns.stop)
        acc_ref[:, there] += product(vec_ref[:, rows], across[0][:, to], across[1][:, to])
        acc_ref[:, rows] += product(vec_ref[:, there], across[2][to, :], across[3][to, :])
    for n in range(panels // 2):
        place = pl.multiple_of((core_ref[0] * (panels // 2) + n) * PANEL, PANEL)
        rows, at = pl.ds(place, PANEL), pl.ds(pl.multiple_of(half + place, PANEL), PANEL)
        acc_ref[:, at] += product(vec_ref[:, rows], far_ref[n, 0], far_ref[n, 1])
        acc_ref[:, rows] += product(vec_ref[:, at], far_ref[n, 2], far_ref[n, 3])
    curve = zero
    for n, (ref, q, at) in enumerate(blocks):
        direction = dir_ref[:, at]
        image = acc_ref[:, at]
        if n < parts:
            image = image + direction / own_ref[cols + 3 : cols + 4, q]
            image_ref[:, at] = image
        else:
            send_ref[:, at.start - half : at.stop - half] = image
        curve = curve + direction * image
    send_ref[:, half:] = curve
    stat_ref[0] = jnp.broadcast_to(step, (cols, LANES))
    stat_ref[1] = jnp.broadcast_to(fresh, (cols, LANES))


def last_kernel(own_ref, dir_ref, res_ref, image_ref, send_ref, come_ref, stat_ref, out_ref):
    cols, half = own_ref.shape[0] - EXTRA, own_ref.shape[1]
    parts = half // LANES
    curve = jnp.sum(send_ref[:, half:] + come_ref[:, half:], axis=1, keepdims=True)
    first = stat_ref[0, :, 0:1]
    step = stat_ref[1, :, 0:1] / curve
    for q in range(parts):
        at = slice(q * LANES, (q + 1) * LANES)
        out_ref[q, 0:cols, :] = first * own_ref[0:cols, at] + step * dir_ref[:, at]
        out_ref[q, cols : 2 * cols, :] = res_ref[:, at] - step * (image_ref[:, at] + come_ref[:, at])


def unpack_kernel(in_ref, sol_hbm, res_hbm, sol_ref, res_ref, sems):
    parts, cols = in_ref.shape[0], in_ref.shape[1] // 2
    copies = []
    for n, (ref, out) in enumerate(((sol_ref, sol_hbm), (res_ref, res_hbm))):
        ref[...] = in_ref[:, n * cols : (n + 1) * cols, :].reshape(parts * cols, LANES).T
        copies.append(pltpu.make_async_copy(ref, out, sems.at[n]))
        copies[-1].start()
    for copy in copies:
        copy.wait()


def shape(*dims, dtype=F32):
    return jax.ShapeDtypeStruct(dims, dtype)


def call(kernel, out, ins, scratch=(), limit=8, where=VM):
    return pl.pallas_call(
        kernel,
        out_shape=out,
        in_specs=ins,
        out_specs=[where] * len(out),
        scratch_shapes=list(scratch),
        compiler_params=pltpu.CompilerParams(vmem_limit_bytes=limit << 20),
    )


def by_columns(positions, radii, right_side):
    row_size, col_size = lax.axis_size("row"), lax.axis_size("col")
    devices = row_size * col_size
    parts = devices // 2
    rows, columns = right_side.shape
    total = rows * devices
    cols = columns // parts
    half = total // 2
    panels = half // PANEL
    kernel_scale, softening = constants(total)
    soft, factor = softening * 4.0**9, kernel_scale * 2.0**9
    groups = [[2 * chip + core for chip in range(parts)] for core in range(2)]
    swap = [(i, i ^ 1) for i in range(col_size)]
    core = (lax.axis_index("col") % 2).astype(jnp.int32).reshape(1)

    (packed,) = call(
        functools.partial(pack_kernel, parts),
        [shape(parts, cols // EXTRA + 1, EXTRA, LANES)],
        [pl.BlockSpec(memory_space=pltpu.HBM)] * 3,
        [
            pltpu.VMEM((3, LANES), F32),
            pltpu.VMEM((1, LANES), F32),
            pltpu.VMEM((LANES, columns), F32),
            pltpu.SemaphoreType.DMA((COPIES + 2,)),
        ],
    )(*[pltpu.with_memory_space_constraint(x, pltpu.HBM) for x in (positions, radii.reshape(1, -1), right_side)])
    own = lax.all_to_all(packed, AXES, 0, 0, axis_index_groups=groups, tiled=True)
    oth = lax.ppermute(own, "col", swap)
    sizes = [sum(cs.stop - cs.start for _, cs, _ in spans(panels)) for spans in (near_spans, across_spans)]
    *near, vec, left, acc, own_flat = call(
        functools.partial(first_kernel, soft, factor),
        [shape(PANEL, sizes[0], dtype=BF16)] * 2
        + [shape(sizes[0] - half, PANEL, dtype=BF16)] * 2
        + [shape(2 * cols, half, dtype=BF16), shape(half, DEPTH, dtype=BF16), shape(cols, half), shape(cols + EXTRA, half)],
        [VM],
        [pltpu.VMEM((DEPTH, half), BF16), pltpu.VMEM((DEPTH, half), F32)],
        16,
    )(own)
    *across, mine, oth_flat = call(
        functools.partial(middle_kernel, soft, factor),
        [shape(PANEL, sizes[1], dtype=BF16)] * 2
        + [shape(sizes[1], PANEL, dtype=BF16)] * 2
        + [shape(panels // 2, 4, PANEL, PANEL, dtype=BF16), shape(cols, total), shape(cols + EXTRA, half)],
        [SM] + [VM] * 5,
        [
            pltpu.VMEM((cols, total), F32),
            pltpu.VMEM((DEPTH, half), BF16),
            pltpu.VMEM((2 * cols, half), BF16),
            pltpu.VMEM((DEPTH, half), F32),
        ],
        8,
    )(core, own_flat, oth, vec, left, acc)
    direction, residual, image, send, stats = call(
        functools.partial(second_kernel, factor),
        [shape(cols, total), shape(cols, half), shape(cols, half), shape(cols, half + LANES), shape(2, cols, LANES)],
        [SM] + [VM] * 13,
        [
            pltpu.VMEM((2 * cols, total), BF16),
            pltpu.VMEM((cols, total), F32),
            pltpu.VMEM((cols, total), F32),
        ],
    )(core, own_flat, oth_flat, mine, lax.ppermute(mine, "col", swap), *near, *across)
    come = lax.ppermute(send, "col", swap)
    (mixed,) = call(last_kernel, [shape(parts, 2 * cols, LANES)], [VM] * 7)(
        own_flat, direction, residual, image, send, come, stats
    )
    mixed = lax.all_to_all(mixed, AXES, 0, 0, axis_index_groups=groups, tiled=True)
    turned = [pltpu.VMEM((LANES, columns), F32)] * 2 + [pltpu.SemaphoreType.DMA((2,))]
    return tuple(call(unpack_kernel, [shape(LANES, columns)] * 2, [VM], turned, where=pl.BlockSpec(memory_space=pltpu.HBM))(mixed))


def body(positions, radii, right_side):
    devices = lax.axis_size("row") * lax.axis_size("col")
    rows, columns = right_side.shape
    total = rows * devices
    fits = rows == LANES and total % (4 * PANEL) == 0 and 16 * devices == 2 * columns
    if fits and 2 * total * total <= KERNEL_BYTES:
        return by_columns(positions, radii, right_side)
    return blockwise(positions, radii, right_side)


def solution(mesh):
    return jax.shard_map(
        body,
        mesh=mesh,
        in_specs=(P(None, ("row", "col")), P(("row", "col")), P(("row", "col"), None)),
        out_specs=(P(("row", "col"), None), P(("row", "col"), None)),
        check_vma=False,
    )
```

```python
import functools

import jax
import jax.numpy as jnp
from jax import lax
from jax.experimental import pallas as pl
from jax.experimental.pallas import tpu as pltpu
from jax.sharding import PartitionSpec as P

ITERS = 2
AXES = ("row", "col")
F32 = jnp.float32
BF16 = jnp.bfloat16
LANES = 128
EXTRA = 4
PANEL = 256
WIDE = 256
DEEP, BROAD = 256, 256
EARLY = 4
AHEAD = 6
COPIES = 4
DEPTH = 48
VM = pl.BlockSpec(memory_space=pltpu.VMEM)
KERNEL_BYTES = 32 << 20


def constants(total):
    kernel_scale = float(total) ** (-0.5)
    spacing = 0.25 * float(total) ** (-1.0 / 3.0)
    return (kernel_scale, spacing * spacing)


def kernel_product(row_points, col_points, values, kernel_scale, softening, limit):
    row_count = row_points.shape[1]
    col_count = col_points.shape[1]
    blocks = max(1, row_count * col_count // limit)
    while row_count % blocks:
        blocks = blocks - 1
    block_size = row_count // blocks
    grouped = row_points.reshape(3, blocks, block_size).transpose(1, 0, 2)

    def apply_block(row_block):
        first = row_block[0][:, None] - col_points[0][None, :]
        second = row_block[1][:, None] - col_points[1][None, :]
        third = row_block[2][:, None] - col_points[2][None, :]
        squared = first * first + second * second + third * third
        weights = lax.rsqrt(squared + softening) * kernel_scale
        return jnp.dot(
            weights, values, preferred_element_type=jnp.float32, precision=lax.Precision.HIGHEST
        )

    return lax.map(apply_block, grouped).reshape(row_count, values.shape[1])


def squares(residual):
    return lax.psum(jnp.sum(residual * residual, axis=0), AXES)


def blockwise(positions, radii, right_side):
    local_count = positions.shape[1]
    total = local_count * lax.axis_size("row") * lax.axis_size("col")
    kernel_scale, softening = constants(total)
    row_points = lax.all_gather(positions, "col", axis=1, tiled=True)
    col_points = lax.all_gather(positions, "row", axis=1, tiled=True)
    limit = 1 << 20
    solution = jnp.zeros_like(right_side)
    residual = right_side
    direction = right_side
    norm_now = squares(residual)
    for iteration in range(ITERS):
        col_values = lax.all_gather(direction, "row", axis=0, tiled=True)
        summed = lax.psum_scatter(
            kernel_product(row_points, col_points, col_values, kernel_scale, softening, limit),
            "col",
            scatter_dimension=0,
            tiled=True,
        )
        image_vec = direction / radii[:, None] + summed
        curvature = lax.psum(jnp.sum(direction * image_vec, axis=0), AXES)
        step_size = norm_now / curvature
        solution = solution + step_size * direction
        residual = residual - step_size * image_vec
        if iteration + 1 < ITERS:
            norm_next = squares(residual)
            direction = residual + norm_next / norm_now * direction
            norm_now = norm_next
    return (solution, residual)


def pack_kernel(parts, pos_hbm, rad_hbm, rhs_hbm, out_ref, pos_ref, rad_ref, rhs_ref, sems):
    rows = [pl.ds(n * (LANES // COPIES), LANES // COPIES) for n in range(COPIES)]
    ends = [(rhs_hbm.at[at], rhs_ref.at[at]) for at in rows] + [(pos_hbm, pos_ref), (rad_hbm, rad_ref)]
    copies = [pltpu.make_async_copy(src, dst, sems.at[n]) for n, (src, dst) in enumerate(ends)]
    for copy in copies:
        copy.start()
    for copy in copies:
        copy.wait()
    cols = rhs_ref.shape[1] // parts
    flipped = rhs_ref[...].T
    extra = jnp.concatenate([pos_ref[...], rad_ref[...]], axis=0)
    for q in range(parts):
        for n in range(cols // EXTRA):
            out_ref[q, n] = flipped[q * cols + n * EXTRA : q * cols + (n + 1) * EXTRA, :]
        out_ref[q, cols // EXTRA] = extra


def split(values):
    high = values.astype(BF16)
    return high, (values - high.astype(F32)).astype(BF16)


def product(vec, high, low):
    cols = vec.shape[0] // 2
    both = jnp.dot(vec, high, preferred_element_type=F32)
    return both[0:cols] + both[cols:] + jnp.dot(vec[0:cols], low, preferred_element_type=F32)


def evaluate(left_ref, right_ref, tasks, ahead):
    begun = []
    for n in range(len(tasks) + ahead):
        if n < len(tasks):
            rows, at, _ = tasks[n]
            begun.append(jnp.dot(left_ref[rows, :], right_ref[:, at], preferred_element_type=F32))
        if n >= ahead:
            tasks[n - ahead][2](*split(lax.rsqrt(begun[n - ahead])))


def pieces(values, count):
    out = []
    for _ in range(count):
        part = values.astype(BF16).astype(F32)
        values = values - part
        out.append(part)
    return out


def factors(flat_ref, soft, fact_ref, right_ref=None, left_ref=None):
    cols = flat_ref.shape[0] - EXTRA
    place = flat_ref[cols : cols + 3, :] * 512.0 - 256.0
    whole = jnp.floor(place + 0.5)
    rest, more = pieces(place - whole, 2)
    both = rest + more
    one = jnp.ones_like(place[0:1])
    norm = pieces(jnp.sum(whole * whole, axis=0, keepdims=True), 3)
    cross = jnp.sum((2.0 * whole + both) * both, axis=0, keepdims=True)

    def write(rows):
        at = 0
        for row in rows:
            fact_ref[at : at + row.shape[0], :] = row
            at += row.shape[0]

    fact_ref[32:, :] = jnp.zeros_like(fact_ref[32:, :])
    twice, less, least = -2.0 * whole, -2.0 * rest, -2.0 * more
    if right_ref is not None:
        write([twice, one, one, one, *norm, one, one, one, *pieces(cross + soft, 3), less, least, twice, twice, less, least, less])
        right_ref[...] = fact_ref[...].astype(BF16)
    if left_ref is not None:
        write([whole, *norm, one, one, one, *pieces(cross, 3), one, one, one, whole, whole, rest, more, rest, rest, more])
        for q in range(flat_ref.shape[1] // LANES):
            at = slice(q * LANES, (q + 1) * LANES)
            left_ref[at, :] = fact_ref[:, at].T.astype(BF16)


def unpack(factor, ref, flat_ref, vec_ref):
    cols = flat_ref.shape[0] - EXTRA
    for q in range(ref.shape[0]):
        at = slice(q * LANES, (q + 1) * LANES)
        flat_ref[:, at] = jnp.concatenate([ref[q, n] for n in range(ref.shape[1])], axis=0)
        high, low = split(flat_ref[0:cols, at] * factor)
        vec_ref[0:cols, at] = high
        vec_ref[cols : 2 * cols, at] = low


def near_spans(panels):
    spans, start = [], 0
    for t in range(panels):
        spans.append((t, slice(t * PANEL, panels * PANEL), start))
        start += (panels - t) * PANEL
    return spans


def first_kernel(soft, factor, own_ref, *refs):
    high_ref, low_ref, high_t_ref, low_t_ref, right_ref, acc_ref, flat_ref, vec_ref, left_ref, fact_ref = refs
    panels = vec_ref.shape[1] // PANEL
    unpack(factor, own_ref, flat_ref, vec_ref)
    factors(flat_ref, soft, fact_ref, right_ref, left_ref)
    acc_ref[...] = jnp.zeros_like(acc_ref)
    tasks = []
    for t, columns, start in near_spans(panels):
        rows = slice(t * PANEL, (t + 1) * PANEL)
        for c in range(columns.start, columns.stop, WIDE):
            at = slice(c, min(c + WIDE, columns.stop))

            def use(high, low, t=t, rows=rows, at=at, to=start + c - columns.start, skip=PANEL if c == columns.start else 0):
                wide = at.stop - at.start
                high_ref[:, to : to + wide] = high
                low_ref[:, to : to + wide] = low
                acc_ref[:, at] += product(vec_ref[:, rows], high, low)
                if wide > skip:
                    high, low = high[:, skip:].T, low[:, skip:].T
                    to = to + skip - (t + 1) * PANEL
                    high_t_ref[to : to + wide - skip, :] = high
                    low_t_ref[to : to + wide - skip, :] = low
                    acc_ref[:, rows] += product(vec_ref[:, at.start + skip : at.stop], high, low)

            tasks.append((rows, at, use))
    evaluate(left_ref, right_ref, tasks, AHEAD)


def middle_kernel(soft, factor, own_ref, oth_ref, right_ref, near_ref, *refs):
    high_ref, low_ref, image_ref, flat_ref, vec_ref, left_ref, fact_ref = refs
    cols, half = own_ref.shape[0] - EXTRA, own_ref.shape[1]
    unpack(factor, oth_ref, flat_ref, vec_ref)
    factors(flat_ref, soft, fact_ref, None, left_ref)
    image_ref[...] = near_ref[...] + own_ref[0:cols, :] / own_ref[cols + 3 : cols + 4, :]
    tasks = []
    for r in range(0, half, DEEP):
        rows = slice(r, r + DEEP)
        for c in range(0, half, BROAD):
            at = slice(c, min(c + BROAD, half))

            def use(high, low, rows=rows, at=at):
                high_ref[rows, at] = high
                low_ref[rows, at] = low
                image_ref[:, at] += product(vec_ref[:, rows], high, low)

            tasks.append((rows, at, use))
    evaluate(left_ref, right_ref, tasks, EARLY)


def near_kernel(factor, image_ref, high_ref, low_ref, high_t_ref, low_t_ref, out_ref, vec_ref):
    cols, half = image_ref.shape
    for c in range(0, half, LANES):
        at = slice(c, c + LANES)
        vec_ref[0:cols, at], vec_ref[cols : 2 * cols, at] = split(image_ref[:, at] * factor)
    out_ref[...] = jnp.zeros_like(out_ref)
    for t, columns, start in near_spans(half // PANEL):
        rows, after = slice(t * PANEL, (t + 1) * PANEL), slice((t + 1) * PANEL, half)
        to = slice(start, start + half - rows.start)
        out_ref[:, columns] += product(vec_ref[:, rows], high_ref[:, to], low_ref[:, to])
        if after.start < half:
            to = slice(start - rows.start, start - rows.start + half - after.start)
            out_ref[:, rows] += product(vec_ref[:, after], high_t_ref[to, :], low_t_ref[to, :])


def second_kernel(factor, own_ref, oth_ref, im_own_ref, im_oth_ref, near_ref, high_ref, low_ref, *refs):
    dir_ref, res_ref, image_ref, curve_ref, stat_ref, vec_ref, acc_ref = refs
    cols, half = im_own_ref.shape
    places = [slice(c, c + LANES) for c in range(0, half, LANES)]
    for at in places:
        vec_ref[0:cols, at], vec_ref[cols : 2 * cols, at] = split(im_oth_ref[:, at] * factor)
    acc_ref[...] = near_ref[...] + im_own_ref[...] / own_ref[cols + 3 : cols + 4, :]
    for r in range(0, half, PANEL):
        rows = slice(r, r + PANEL)
        acc_ref[...] += product(vec_ref[:, rows], high_ref[rows, :], low_ref[rows, :])
    blocks = [(ref, im, at) for ref, im in ((own_ref, im_own_ref), (oth_ref, im_oth_ref)) for at in places]
    zero = jnp.zeros((cols, LANES), F32)
    norm, curve, fresh = zero, zero, zero
    for ref, im, at in blocks:
        value = ref[0:cols, at]
        norm = norm + value * value
        curve = curve + value * im[:, at]
    norm = jnp.sum(norm, axis=1, keepdims=True)
    step = norm / jnp.sum(curve, axis=1, keepdims=True)
    for ref, im, at in blocks:
        value = ref[0:cols, at] - step * im[:, at]
        fresh = fresh + value * value
    fresh = jnp.sum(fresh, axis=1, keepdims=True)
    ratio = fresh / norm
    curve = zero
    for at in places:
        value, first = own_ref[0:cols, at], im_own_ref[:, at]
        left = value - step * first
        direction = left + ratio * value
        image = first + (ratio * first - step * acc_ref[:, at])
        res_ref[:, at] = left
        dir_ref[:, at] = direction
        image_ref[:, at] = image
        curve = curve + direction * image
    curve_ref[...] = curve
    stat_ref[0] = jnp.broadcast_to(step, (cols, LANES))
    stat_ref[1] = jnp.broadcast_to(fresh, (cols, LANES))


def last_kernel(own_ref, dir_ref, res_ref, image_ref, curve_ref, other_ref, stat_ref, out_ref):
    cols, half = own_ref.shape[0] - EXTRA, own_ref.shape[1]
    parts = half // LANES
    curve = jnp.sum(curve_ref[...] + other_ref[...], axis=1, keepdims=True)
    first = stat_ref[0, :, 0:1]
    step = stat_ref[1, :, 0:1] / curve
    for q in range(parts):
        at = slice(q * LANES, (q + 1) * LANES)
        out_ref[q, 0:cols, :] = first * own_ref[0:cols, at] + step * dir_ref[:, at]
        out_ref[q, cols : 2 * cols, :] = res_ref[:, at] - step * image_ref[:, at]


def unpack_kernel(in_ref, sol_hbm, res_hbm, sol_ref, res_ref, sems):
    parts, cols = in_ref.shape[0], in_ref.shape[1] // 2
    copies = []
    for n, (ref, out) in enumerate(((sol_ref, sol_hbm), (res_ref, res_hbm))):
        ref[...] = in_ref[:, n * cols : (n + 1) * cols, :].reshape(parts * cols, LANES).T
        copies.append(pltpu.make_async_copy(ref, out, sems.at[n]))
        copies[-1].start()
    for copy in copies:
        copy.wait()


def shape(*dims, dtype=F32):
    return jax.ShapeDtypeStruct(dims, dtype)


def call(kernel, out, ins, scratch=(), limit=8, where=VM):
    return pl.pallas_call(
        kernel,
        out_shape=out,
        in_specs=ins,
        out_specs=[where] * len(out),
        scratch_shapes=list(scratch),
        compiler_params=pltpu.CompilerParams(vmem_limit_bytes=limit << 20),
    )


def by_columns(positions, radii, right_side):
    row_size, col_size = lax.axis_size("row"), lax.axis_size("col")
    devices = row_size * col_size
    parts = devices // 2
    rows, columns = right_side.shape
    total = rows * devices
    cols = columns // parts
    half = total // 2
    panels = half // PANEL
    kernel_scale, softening = constants(total)
    soft, factor = softening * 4.0**9, kernel_scale * 2.0**9
    groups = [[2 * chip + core for chip in range(parts)] for core in range(2)]
    swap = [(i, i ^ 1) for i in range(col_size)]

    (packed,) = call(
        functools.partial(pack_kernel, parts),
        [shape(parts, cols // EXTRA + 1, EXTRA, LANES)],
        [pl.BlockSpec(memory_space=pltpu.HBM)] * 3,
        [
            pltpu.VMEM((3, LANES), F32),
            pltpu.VMEM((1, LANES), F32),
            pltpu.VMEM((LANES, columns), F32),
            pltpu.SemaphoreType.DMA((COPIES + 2,)),
        ],
    )(*[pltpu.with_memory_space_constraint(x, pltpu.HBM) for x in (positions, radii.reshape(1, -1), right_side)])
    own = lax.all_to_all(packed, AXES, 0, 0, axis_index_groups=groups, tiled=True)
    oth = lax.ppermute(own, "col", swap)
    size = sum(cs.stop - cs.start for _, cs, _ in near_spans(panels))
    *near, right, acc, own_flat = call(
        functools.partial(first_kernel, soft, factor),
        [shape(PANEL, size, dtype=BF16)] * 2
        + [shape(size - half, PANEL, dtype=BF16)] * 2
        + [shape(DEPTH, half, dtype=BF16), shape(cols, half), shape(cols + EXTRA, half)],
        [VM],
        [
            pltpu.VMEM((2 * cols, half), BF16),
            pltpu.VMEM((half, DEPTH), BF16),
            pltpu.VMEM((DEPTH, half), F32),
        ],
        16,
    )(own)
    *across, image, oth_flat = call(
        functools.partial(middle_kernel, soft, factor),
        [shape(half, half, dtype=BF16)] * 2 + [shape(cols, half), shape(cols + EXTRA, half)],
        [VM] * 4,
        [
            pltpu.VMEM((2 * cols, half), BF16),
            pltpu.VMEM((half, DEPTH), BF16),
            pltpu.VMEM((DEPTH, half), F32),
        ],
        10,
    )(own_flat, oth, right, acc)
    image_oth = lax.ppermute(image, "col", swap)
    vec = pltpu.VMEM((2 * cols, half), BF16)
    (begun,) = call(functools.partial(near_kernel, factor), [shape(cols, half)], [VM] * 5, [vec])(image, *near)
    direction, residual, second, curve, stats = call(
        functools.partial(second_kernel, factor),
        [shape(cols, half)] * 3 + [shape(cols, LANES), shape(2, cols, LANES)],
        [VM] * 7,
        [vec, pltpu.VMEM((cols, half), F32)],
    )(own_flat, oth_flat, image, image_oth, begun, *across)
    (mixed,) = call(last_kernel, [shape(parts, 2 * cols, LANES)], [VM] * 7)(
        own_flat, direction, residual, second, curve, lax.ppermute(curve, "col", swap), stats
    )
    mixed = lax.all_to_all(mixed, AXES, 0, 0, axis_index_groups=groups, tiled=True)
    turned = [pltpu.VMEM((LANES, columns), F32)] * 2 + [pltpu.SemaphoreType.DMA((2,))]
    return tuple(call(unpack_kernel, [shape(LANES, columns)] * 2, [VM], turned, where=pl.BlockSpec(memory_space=pltpu.HBM))(mixed))


def body(positions, radii, right_side):
    devices = lax.axis_size("row") * lax.axis_size("col")
    rows, columns = right_side.shape
    total = rows * devices
    fits = rows == LANES and total % (4 * PANEL) == 0 and 16 * devices == 2 * columns
    if fits and 2 * total * total <= KERNEL_BYTES:
        return by_columns(positions, radii, right_side)
    return blockwise(positions, radii, right_side)


def solution(mesh):
    return jax.shard_map(
        body,
        mesh=mesh,
        in_specs=(P(None, ("row", "col")), P(("row", "col")), P(("row", "col"), None)),
        out_specs=(P(("row", "col"), None), P(("row", "col"), None)),
        check_vma=False,
    )
```

```python
import functools

import jax
import jax.numpy as jnp
from jax import lax
from jax.experimental import pallas as pl
from jax.experimental.pallas import tpu as pltpu
from jax.sharding import PartitionSpec as P

ITERS = 2
AXES = ("row", "col")
F32 = jnp.float32
BF16 = jnp.bfloat16
LANES = 128
EXTRA = 4
PANEL = 256
WIDE = 256
DEEP, BROAD = 256, 256
EARLY = 4
AHEAD = 6
COPIES = 4
DEPTH = 48
VM = pl.BlockSpec(memory_space=pltpu.VMEM)
KERNEL_BYTES = 32 << 20


def constants(total):
    kernel_scale = float(total) ** (-0.5)
    spacing = 0.25 * float(total) ** (-1.0 / 3.0)
    return (kernel_scale, spacing * spacing)


def kernel_product(row_points, col_points, values, kernel_scale, softening, limit):
    row_count = row_points.shape[1]
    col_count = col_points.shape[1]
    blocks = max(1, row_count * col_count // limit)
    while row_count % blocks:
        blocks = blocks - 1
    block_size = row_count // blocks
    grouped = row_points.reshape(3, blocks, block_size).transpose(1, 0, 2)

    def apply_block(row_block):
        first = row_block[0][:, None] - col_points[0][None, :]
        second = row_block[1][:, None] - col_points[1][None, :]
        third = row_block[2][:, None] - col_points[2][None, :]
        squared = first * first + second * second + third * third
        weights = lax.rsqrt(squared + softening) * kernel_scale
        return jnp.dot(
            weights, values, preferred_element_type=jnp.float32, precision=lax.Precision.HIGHEST
        )

    return lax.map(apply_block, grouped).reshape(row_count, values.shape[1])


def squares(residual):
    return lax.psum(jnp.sum(residual * residual, axis=0), AXES)


def blockwise(positions, radii, right_side):
    local_count = positions.shape[1]
    total = local_count * lax.axis_size("row") * lax.axis_size("col")
    kernel_scale, softening = constants(total)
    row_points = lax.all_gather(positions, "col", axis=1, tiled=True)
    col_points = lax.all_gather(positions, "row", axis=1, tiled=True)
    limit = 1 << 20
    solution = jnp.zeros_like(right_side)
    residual = right_side
    direction = right_side
    norm_now = squares(residual)
    for iteration in range(ITERS):
        col_values = lax.all_gather(direction, "row", axis=0, tiled=True)
        summed = lax.psum_scatter(
            kernel_product(row_points, col_points, col_values, kernel_scale, softening, limit),
            "col",
            scatter_dimension=0,
            tiled=True,
        )
        image_vec = direction / radii[:, None] + summed
        curvature = lax.psum(jnp.sum(direction * image_vec, axis=0), AXES)
        step_size = norm_now / curvature
        solution = solution + step_size * direction
        residual = residual - step_size * image_vec
        if iteration + 1 < ITERS:
            norm_next = squares(residual)
            direction = residual + norm_next / norm_now * direction
            norm_now = norm_next
    return (solution, residual)


def pack_kernel(parts, pos_hbm, rad_hbm, rhs_hbm, out_ref, pos_ref, rad_ref, rhs_ref, sems):
    rows = [pl.ds(n * (LANES // COPIES), LANES // COPIES) for n in range(COPIES)]
    ends = [(rhs_hbm.at[at], rhs_ref.at[at]) for at in rows] + [(pos_hbm, pos_ref), (rad_hbm, rad_ref)]
    copies = [pltpu.make_async_copy(src, dst, sems.at[n]) for n, (src, dst) in enumerate(ends)]
    for copy in copies:
        copy.start()
    for copy in copies:
        copy.wait()
    cols = rhs_ref.shape[1] // parts
    flipped = rhs_ref[...].T
    extra = jnp.concatenate([pos_ref[...], rad_ref[...]], axis=0)
    for q in range(parts):
        for n in range(cols // EXTRA):
            out_ref[q, n] = flipped[q * cols + n * EXTRA : q * cols + (n + 1) * EXTRA, :]
        out_ref[q, cols // EXTRA] = extra


def split(values):
    high = values.astype(BF16)
    return high, (values - high.astype(F32)).astype(BF16)


def product(vec, high, low):
    cols = vec.shape[0] // 2
    both = jnp.dot(vec, high, preferred_element_type=F32)
    return both[0:cols] + both[cols:] + jnp.dot(vec[0:cols], low, preferred_element_type=F32)


def evaluate(left_ref, right_ref, tasks, ahead):
    begun = []
    for n in range(len(tasks) + ahead):
        if n < len(tasks):
            rows, at, _, prepare = tasks[n]
            if prepare is not None:
                prepare()
            begun.append(jnp.dot(left_ref[rows, :], right_ref[:, at], preferred_element_type=F32))
        if n >= ahead:
            tasks[n - ahead][2](*split(lax.rsqrt(begun[n - ahead])))


def pieces(values, count):
    out = []
    for _ in range(count):
        part = values.astype(BF16).astype(F32)
        values = values - part
        out.append(part)
    return out


def factors(flat_ref, at, soft, fact_ref, right_ref=None, left_ref=None):
    cols = flat_ref.shape[0] - EXTRA
    place = flat_ref[cols : cols + 3, at] * 512.0 - 256.0
    whole = jnp.floor(place + 0.5)
    rest, more = pieces(place - whole, 2)
    both = rest + more
    one = jnp.ones_like(place[0:1])
    norm = pieces(jnp.sum(whole * whole, axis=0, keepdims=True), 3)
    cross = jnp.sum((2.0 * whole + both) * both, axis=0, keepdims=True)

    def write(rows):
        place = 0
        for row in rows:
            fact_ref[place : place + row.shape[0], at] = row
            place += row.shape[0]

    fact_ref[32:, at] = jnp.zeros_like(fact_ref[32:, at])
    twice, less, least = -2.0 * whole, -2.0 * rest, -2.0 * more
    if right_ref is not None:
        write([twice, one, one, one, *norm, one, one, one, *pieces(cross + soft, 3), less, least, twice, twice, less, least, less])
        right_ref[:, at] = fact_ref[:, at].astype(BF16)
    if left_ref is not None:
        write([whole, *norm, one, one, one, *pieces(cross, 3), one, one, one, whole, whole, rest, more, rest, rest, more])
        for q in range(at.start, at.stop, LANES):
            left_ref[q : q + LANES, :] = fact_ref[:, q : q + LANES].T.astype(BF16)


def unpack(factor, ref, span, flat_ref, vec_ref):
    cols = flat_ref.shape[0] - EXTRA
    for q in range(span.start // LANES, span.stop // LANES):
        at = slice(q * LANES, (q + 1) * LANES)
        flat_ref[:, at] = jnp.concatenate([ref[q, n] for n in range(ref.shape[1])], axis=0)
        high, low = split(flat_ref[0:cols, at] * factor)
        vec_ref[0:cols, at] = high
        vec_ref[cols : 2 * cols, at] = low


def near_spans(panels):
    spans, start = [], 0
    for t in range(panels):
        spans.append((t, slice(t * PANEL, panels * PANEL), start))
        start += (panels - t) * PANEL
    return spans


def first_kernel(soft, factor, own_ref, *refs):
    high_ref, low_ref, high_t_ref, low_t_ref, right_ref, acc_ref, flat_ref, vec_ref, left_ref, fact_ref = refs
    panels = vec_ref.shape[1] // PANEL
    acc_ref[...] = jnp.zeros_like(acc_ref)
    tasks = []
    whole = slice(0, panels * PANEL)
    unpack(factor, own_ref, whole, flat_ref, vec_ref)
    factors(flat_ref, whole, soft, fact_ref, right_ref, left_ref)
    for t, columns, start in near_spans(panels):
        rows = slice(t * PANEL, (t + 1) * PANEL)
        for c in range(columns.start, columns.stop, WIDE):
            at = slice(c, min(c + WIDE, columns.stop))

            def use(high, low, t=t, rows=rows, at=at, to=start + c - columns.start, skip=PANEL if c == columns.start else 0):
                wide = at.stop - at.start
                high_ref[:, to : to + wide] = high
                low_ref[:, to : to + wide] = low
                acc_ref[:, at] += product(vec_ref[:, rows], high, low)
                if wide > skip:
                    high, low = high[:, skip:].T, low[:, skip:].T
                    to = to + skip - (t + 1) * PANEL
                    high_t_ref[to : to + wide - skip, :] = high
                    low_t_ref[to : to + wide - skip, :] = low
                    acc_ref[:, rows] += product(vec_ref[:, at.start + skip : at.stop], high, low)

            tasks.append((rows, at, use, None))
    evaluate(left_ref, right_ref, tasks, AHEAD)


def middle_kernel(soft, factor, own_ref, oth_ref, right_ref, near_ref, *refs):
    high_ref, low_ref, image_ref, flat_ref, vec_ref, left_ref, fact_ref = refs
    cols, half = own_ref.shape[0] - EXTRA, own_ref.shape[1]
    image_ref[...] = near_ref[...] + own_ref[0:cols, :] / own_ref[cols + 3 : cols + 4, :]
    tasks = []
    for r in range(0, half, DEEP):
        rows = slice(r, r + DEEP)

        def prepare(rows=rows):
            unpack(factor, oth_ref, rows, flat_ref, vec_ref)
            factors(flat_ref, rows, soft, fact_ref, None, left_ref)

        for c in range(0, half, BROAD):
            at = slice(c, min(c + BROAD, half))

            def use(high, low, rows=rows, at=at):
                high_ref[rows, at] = high
                low_ref[rows, at] = low
                image_ref[:, at] += product(vec_ref[:, rows], high, low)

            tasks.append((rows, at, use, prepare if c == 0 else None))
    evaluate(left_ref, right_ref, tasks, EARLY)


def near_kernel(factor, image_ref, high_ref, low_ref, high_t_ref, low_t_ref, out_ref, vec_ref):
    cols, half = image_ref.shape
    for c in range(0, half, LANES):
        at = slice(c, c + LANES)
        vec_ref[0:cols, at], vec_ref[cols : 2 * cols, at] = split(image_ref[:, at] * factor)
    out_ref[...] = jnp.zeros_like(out_ref)
    for t, columns, start in near_spans(half // PANEL):
        rows, after = slice(t * PANEL, (t + 1) * PANEL), slice((t + 1) * PANEL, half)
        to = slice(start, start + half - rows.start)
        out_ref[:, columns] += product(vec_ref[:, rows], high_ref[:, to], low_ref[:, to])
        if after.start < half:
            to = slice(start - rows.start, start - rows.start + half - after.start)
            out_ref[:, rows] += product(vec_ref[:, after], high_t_ref[to, :], low_t_ref[to, :])


def second_kernel(factor, own_ref, oth_ref, im_own_ref, im_oth_ref, near_ref, high_ref, low_ref, *refs):
    dir_ref, res_ref, image_ref, curve_ref, stat_ref, vec_ref, acc_ref = refs
    cols, half = im_own_ref.shape
    places = [slice(c, c + LANES) for c in range(0, half, LANES)]
    for at in places:
        vec_ref[0:cols, at], vec_ref[cols : 2 * cols, at] = split(im_oth_ref[:, at] * factor)
    acc_ref[...] = near_ref[...] + im_own_ref[...] / own_ref[cols + 3 : cols + 4, :]
    for r in range(0, half, PANEL):
        rows = slice(r, r + PANEL)
        acc_ref[...] += product(vec_ref[:, rows], high_ref[rows, :], low_ref[rows, :])
    blocks = [(ref, im, at) for ref, im in ((own_ref, im_own_ref), (oth_ref, im_oth_ref)) for at in places]
    zero = jnp.zeros((cols, LANES), F32)
    norm, curve, fresh = zero, zero, zero
    for ref, im, at in blocks:
        value = ref[0:cols, at]
        norm = norm + value * value
        curve = curve + value * im[:, at]
    norm = jnp.sum(norm, axis=1, keepdims=True)
    step = norm / jnp.sum(curve, axis=1, keepdims=True)
    for ref, im, at in blocks:
        value = ref[0:cols, at] - step * im[:, at]
        fresh = fresh + value * value
    fresh = jnp.sum(fresh, axis=1, keepdims=True)
    ratio = fresh / norm
    curve = zero
    for at in places:
        value, first = own_ref[0:cols, at], im_own_ref[:, at]
        left = value - step * first
        direction = left + ratio * value
        image = first + (ratio * first - step * acc_ref[:, at])
        res_ref[:, at] = left
        dir_ref[:, at] = direction
        image_ref[:, at] = image
        curve = curve + direction * image
    curve_ref[...] = curve
    stat_ref[0] = jnp.broadcast_to(step, (cols, LANES))
    stat_ref[1] = jnp.broadcast_to(fresh, (cols, LANES))


def last_kernel(own_ref, dir_ref, res_ref, image_ref, curve_ref, other_ref, stat_ref, out_ref):
    cols, half = own_ref.shape[0] - EXTRA, own_ref.shape[1]
    parts = half // LANES
    curve = jnp.sum(curve_ref[...] + other_ref[...], axis=1, keepdims=True)
    first = stat_ref[0, :, 0:1]
    step = stat_ref[1, :, 0:1] / curve
    for q in range(parts):
        at = slice(q * LANES, (q + 1) * LANES)
        out_ref[q, 0:cols, :] = first * own_ref[0:cols, at] + step * dir_ref[:, at]
        out_ref[q, cols : 2 * cols, :] = res_ref[:, at] - step * image_ref[:, at]


def unpack_kernel(in_ref, sol_hbm, res_hbm, sol_ref, res_ref, sems):
    parts, cols = in_ref.shape[0], in_ref.shape[1] // 2
    copies = []
    for n, (ref, out) in enumerate(((sol_ref, sol_hbm), (res_ref, res_hbm))):
        ref[...] = in_ref[:, n * cols : (n + 1) * cols, :].reshape(parts * cols, LANES).T
        copies.append(pltpu.make_async_copy(ref, out, sems.at[n]))
        copies[-1].start()
    for copy in copies:
        copy.wait()


def shape(*dims, dtype=F32):
    return jax.ShapeDtypeStruct(dims, dtype)


def call(kernel, out, ins, scratch=(), limit=8, where=VM):
    return pl.pallas_call(
        kernel,
        out_shape=out,
        in_specs=ins,
        out_specs=[where] * len(out),
        scratch_shapes=list(scratch),
        compiler_params=pltpu.CompilerParams(vmem_limit_bytes=limit << 20),
    )


def by_columns(positions, radii, right_side):
    row_size, col_size = lax.axis_size("row"), lax.axis_size("col")
    devices = row_size * col_size
    parts = devices // 2
    rows, columns = right_side.shape
    total = rows * devices
    cols = columns // parts
    half = total // 2
    panels = half // PANEL
    kernel_scale, softening = constants(total)
    soft, factor = softening * 4.0**9, kernel_scale * 2.0**9
    groups = [[2 * chip + core for chip in range(parts)] for core in range(2)]
    swap = [(i, i ^ 1) for i in range(col_size)]

    (packed,) = call(
        functools.partial(pack_kernel, parts),
        [shape(parts, cols // EXTRA + 1, EXTRA, LANES)],
        [pl.BlockSpec(memory_space=pltpu.HBM)] * 3,
        [
            pltpu.VMEM((3, LANES), F32),
            pltpu.VMEM((1, LANES), F32),
            pltpu.VMEM((LANES, columns), F32),
            pltpu.SemaphoreType.DMA((COPIES + 2,)),
        ],
    )(*[pltpu.with_memory_space_constraint(x, pltpu.HBM) for x in (positions, radii.reshape(1, -1), right_side)])
    own = lax.all_to_all(packed, AXES, 0, 0, axis_index_groups=groups, tiled=True)
    oth = lax.ppermute(own, "col", swap)
    size = sum(cs.stop - cs.start for _, cs, _ in near_spans(panels))
    *near, right, acc, own_flat = call(
        functools.partial(first_kernel, soft, factor),
        [shape(PANEL, size, dtype=BF16)] * 2
        + [shape(size - half, PANEL, dtype=BF16)] * 2
        + [shape(DEPTH, half, dtype=BF16), shape(cols, half), shape(cols + EXTRA, half)],
        [VM],
        [
            pltpu.VMEM((2 * cols, half), BF16),
            pltpu.VMEM((half, DEPTH), BF16),
            pltpu.VMEM((DEPTH, half), F32),
        ],
        16,
    )(own)
    *across, image, oth_flat = call(
        functools.partial(middle_kernel, soft, factor),
        [shape(half, half, dtype=BF16)] * 2 + [shape(cols, half), shape(cols + EXTRA, half)],
        [VM] * 4,
        [
            pltpu.VMEM((2 * cols, half), BF16),
            pltpu.VMEM((half, DEPTH), BF16),
            pltpu.VMEM((DEPTH, half), F32),
        ],
        10,
    )(own_flat, oth, right, acc)
    image_oth = lax.ppermute(image, "col", swap)
    vec = pltpu.VMEM((2 * cols, half), BF16)
    (begun,) = call(functools.partial(near_kernel, factor), [shape(cols, half)], [VM] * 5, [vec])(image, *near)
    direction, residual, second, curve, stats = call(
        functools.partial(second_kernel, factor),
        [shape(cols, half)] * 3 + [shape(cols, LANES), shape(2, cols, LANES)],
        [VM] * 7,
        [vec, pltpu.VMEM((cols, half), F32)],
    )(own_flat, oth_flat, image, image_oth, begun, *across)
    (mixed,) = call(last_kernel, [shape(parts, 2 * cols, LANES)], [VM] * 7)(
        own_flat, direction, residual, second, curve, lax.ppermute(curve, "col", swap), stats
    )
    mixed = lax.all_to_all(mixed, AXES, 0, 0, axis_index_groups=groups, tiled=True)
    turned = [pltpu.VMEM((LANES, columns), F32)] * 2 + [pltpu.SemaphoreType.DMA((2,))]
    return tuple(call(unpack_kernel, [shape(LANES, columns)] * 2, [VM], turned, where=pl.BlockSpec(memory_space=pltpu.HBM))(mixed))


def body(positions, radii, right_side):
    devices = lax.axis_size("row") * lax.axis_size("col")
    rows, columns = right_side.shape
    total = rows * devices
    fits = rows == LANES and total % (4 * PANEL) == 0 and 16 * devices == 2 * columns
    if fits and 2 * total * total <= KERNEL_BYTES:
        return by_columns(positions, radii, right_side)
    return blockwise(positions, radii, right_side)


def solution(mesh):
    return jax.shard_map(
        body,
        mesh=mesh,
        in_specs=(P(None, ("row", "col")), P(("row", "col")), P(("row", "col"), None)),
        out_specs=(P(("row", "col"), None), P(("row", "col"), None)),
        check_vma=False,
    )
```

```python
import functools

import jax
import jax.numpy as jnp
from jax import lax
from jax.experimental import pallas as pl
from jax.experimental.pallas import tpu as pltpu
from jax.sharding import PartitionSpec as P

ITERS = 2
AXES = ("row", "col")
F32 = jnp.float32
BF16 = jnp.bfloat16
LANES = 128
EXTRA = 4
PANEL = 256
WIDE = 256
DEEP, BROAD = 256, 256
EARLY = 4
AHEAD = 6
COPIES = 4
DEPTH = 48
VM = pl.BlockSpec(memory_space=pltpu.VMEM)
KERNEL_BYTES = 32 << 20


def constants(total):
    kernel_scale = float(total) ** (-0.5)
    spacing = 0.25 * float(total) ** (-1.0 / 3.0)
    return (kernel_scale, spacing * spacing)


def kernel_product(row_points, col_points, values, kernel_scale, softening, limit):
    row_count = row_points.shape[1]
    col_count = col_points.shape[1]
    blocks = max(1, row_count * col_count // limit)
    while row_count % blocks:
        blocks = blocks - 1
    block_size = row_count // blocks
    grouped = row_points.reshape(3, blocks, block_size).transpose(1, 0, 2)

    def apply_block(row_block):
        first = row_block[0][:, None] - col_points[0][None, :]
        second = row_block[1][:, None] - col_points[1][None, :]
        third = row_block[2][:, None] - col_points[2][None, :]
        squared = first * first + second * second + third * third
        weights = lax.rsqrt(squared + softening) * kernel_scale
        return jnp.dot(
            weights, values, preferred_element_type=jnp.float32, precision=lax.Precision.HIGHEST
        )

    return lax.map(apply_block, grouped).reshape(row_count, values.shape[1])


def squares(residual):
    return lax.psum(jnp.sum(residual * residual, axis=0), AXES)


def blockwise(positions, radii, right_side):
    local_count = positions.shape[1]
    total = local_count * lax.axis_size("row") * lax.axis_size("col")
    kernel_scale, softening = constants(total)
    row_points = lax.all_gather(positions, "col", axis=1, tiled=True)
    col_points = lax.all_gather(positions, "row", axis=1, tiled=True)
    limit = 1 << 20
    solution = jnp.zeros_like(right_side)
    residual = right_side
    direction = right_side
    norm_now = squares(residual)
    for iteration in range(ITERS):
        col_values = lax.all_gather(direction, "row", axis=0, tiled=True)
        summed = lax.psum_scatter(
            kernel_product(row_points, col_points, col_values, kernel_scale, softening, limit),
            "col",
            scatter_dimension=0,
            tiled=True,
        )
        image_vec = direction / radii[:, None] + summed
        curvature = lax.psum(jnp.sum(direction * image_vec, axis=0), AXES)
        step_size = norm_now / curvature
        solution = solution + step_size * direction
        residual = residual - step_size * image_vec
        if iteration + 1 < ITERS:
            norm_next = squares(residual)
            direction = residual + norm_next / norm_now * direction
            norm_now = norm_next
    return (solution, residual)


def pack_kernel(parts, pos_hbm, rad_hbm, rhs_hbm, out_ref, pos_ref, rad_ref, rhs_ref, sems):
    rows = [pl.ds(n * (LANES // COPIES), LANES // COPIES) for n in range(COPIES)]
    ends = [(rhs_hbm.at[at], rhs_ref.at[at]) for at in rows] + [(pos_hbm, pos_ref), (rad_hbm, rad_ref)]
    copies = [pltpu.make_async_copy(src, dst, sems.at[n]) for n, (src, dst) in enumerate(ends)]
    for copy in copies:
        copy.start()
    for copy in copies:
        copy.wait()
    cols = rhs_ref.shape[1] // parts
    flipped = rhs_ref[...].T
    extra = jnp.concatenate([pos_ref[...], rad_ref[...]], axis=0)
    for q in range(parts):
        for n in range(cols // EXTRA):
            out_ref[q, n] = flipped[q * cols + n * EXTRA : q * cols + (n + 1) * EXTRA, :]
        out_ref[q, cols // EXTRA] = extra


def split(values):
    high = values.astype(BF16)
    return high, (values - high.astype(F32)).astype(BF16)


def product(vec, high, low):
    cols = vec.shape[0] // 2
    both = jnp.dot(vec, high, preferred_element_type=F32)
    return both[0:cols] + both[cols:] + jnp.dot(vec[0:cols], low, preferred_element_type=F32)


def evaluate(left_ref, right_ref, tasks, ahead):
    begun = []
    for n in range(len(tasks) + ahead):
        if n < len(tasks):
            rows, at, _, prepare = tasks[n]
            if prepare is not None:
                prepare()
            begun.append(jnp.dot(left_ref[rows, :], right_ref[:, at], preferred_element_type=F32))
        if n >= ahead:
            tasks[n - ahead][2](*split(lax.rsqrt(begun[n - ahead])))


def pieces(values, count):
    out = []
    for _ in range(count):
        part = values.astype(BF16).astype(F32)
        values = values - part
        out.append(part)
    return out


def factors(flat_ref, at, soft, fact_ref, right_ref=None, left_ref=None):
    cols = flat_ref.shape[0] - EXTRA
    place = flat_ref[cols : cols + 3, at] * 512.0 - 256.0
    whole = jnp.floor(place + 0.5)
    rest, more = pieces(place - whole, 2)
    both = rest + more
    one = jnp.ones_like(place[0:1])
    norm = pieces(jnp.sum(whole * whole, axis=0, keepdims=True), 3)
    cross = jnp.sum((2.0 * whole + both) * both, axis=0, keepdims=True)

    def write(rows):
        place = 0
        for row in rows:
            fact_ref[place : place + row.shape[0], at] = row
            place += row.shape[0]

    fact_ref[32:, at] = jnp.zeros_like(fact_ref[32:, at])
    twice, less, least = -2.0 * whole, -2.0 * rest, -2.0 * more
    if right_ref is not None:
        write([twice, one, one, one, *norm, one, one, one, *pieces(cross + soft, 3), less, least, twice, twice, less, least, less])
        right_ref[:, at] = fact_ref[:, at].astype(BF16)
    if left_ref is not None:
        write([whole, *norm, one, one, one, *pieces(cross, 3), one, one, one, whole, whole, rest, more, rest, rest, more])
        for q in range(at.start, at.stop, LANES):
            left_ref[q : q + LANES, :] = fact_ref[:, q : q + LANES].T.astype(BF16)


def unpack(factor, ref, span, flat_ref, vec_ref):
    cols = flat_ref.shape[0] - EXTRA
    for q in range(span.start // LANES, span.stop // LANES):
        at = slice(q * LANES, (q + 1) * LANES)
        flat_ref[:, at] = jnp.concatenate([ref[q, n] for n in range(ref.shape[1])], axis=0)
        high, low = split(flat_ref[0:cols, at] * factor)
        vec_ref[0:cols, at] = high
        vec_ref[cols : 2 * cols, at] = low


def near_spans(panels):
    spans, start = [], 0
    for t in range(panels):
        spans.append((t, slice(t * PANEL, panels * PANEL), start))
        start += (panels - t) * PANEL
    return spans


def first_kernel(soft, factor, own_ref, *refs):
    high_ref, low_ref, high_t_ref, low_t_ref, right_ref, acc_ref, flat_ref, vec_ref, left_ref, fact_ref = refs
    panels = vec_ref.shape[1] // PANEL
    acc_ref[...] = jnp.zeros_like(acc_ref)
    tasks = []
    whole = slice(0, panels * PANEL)
    unpack(factor, own_ref, whole, flat_ref, vec_ref)
    factors(flat_ref, whole, soft, fact_ref, right_ref, left_ref)
    for t, columns, start in near_spans(panels):
        rows = slice(t * PANEL, (t + 1) * PANEL)
        for c in range(columns.start, columns.stop, WIDE):
            at = slice(c, min(c + WIDE, columns.stop))

            def use(high, low, t=t, rows=rows, at=at, to=start + c - columns.start, skip=PANEL if c == columns.start else 0):
                wide = at.stop - at.start
                high_ref[:, to : to + wide] = high
                low_ref[:, to : to + wide] = low
                acc_ref[:, at] += product(vec_ref[:, rows], high, low)
                if wide > skip:
                    high, low = high[:, skip:].T, low[:, skip:].T
                    to = to + skip - (t + 1) * PANEL
                    high_t_ref[to : to + wide - skip, :] = high
                    low_t_ref[to : to + wide - skip, :] = low
                    acc_ref[:, rows] += product(vec_ref[:, at.start + skip : at.stop], high, low)

            tasks.append((rows, at, use, None))
    evaluate(left_ref, right_ref, tasks, AHEAD)


def middle_kernel(soft, factor, own_ref, oth_ref, right_ref, near_ref, *refs):
    high_ref, low_ref, image_ref, flat_ref, vec_ref, left_ref, fact_ref = refs
    cols, half = own_ref.shape[0] - EXTRA, own_ref.shape[1]
    image_ref[...] = near_ref[...] + own_ref[0:cols, :] / own_ref[cols + 3 : cols + 4, :]
    tasks = []
    for r in range(0, half, DEEP):
        rows = slice(r, r + DEEP)

        def prepare(rows=rows):
            unpack(factor, oth_ref, rows, flat_ref, vec_ref)
            factors(flat_ref, rows, soft, fact_ref, None, left_ref)

        for c in range(0, half, BROAD):
            at = slice(c, min(c + BROAD, half))

            def use(high, low, rows=rows, at=at):
                high_ref[rows, at] = high
                low_ref[rows, at] = low
                image_ref[:, at] += product(vec_ref[:, rows], high, low)

            tasks.append((rows, at, use, prepare if c == 0 else None))
    evaluate(left_ref, right_ref, tasks, EARLY)


def near_kernel(factor, image_ref, high_ref, low_ref, high_t_ref, low_t_ref, out_ref, vec_ref):
    cols, half = image_ref.shape
    for c in range(0, half, LANES):
        at = slice(c, c + LANES)
        vec_ref[0:cols, at], vec_ref[cols : 2 * cols, at] = split(image_ref[:, at] * factor)
    out_ref[...] = jnp.zeros_like(out_ref)
    for t, columns, start in near_spans(half // PANEL):
        rows, after = slice(t * PANEL, (t + 1) * PANEL), slice((t + 1) * PANEL, half)
        to = slice(start, start + half - rows.start)
        out_ref[:, columns] += product(vec_ref[:, rows], high_ref[:, to], low_ref[:, to])
        if after.start < half:
            to = slice(start - rows.start, start - rows.start + half - after.start)
            out_ref[:, rows] += product(vec_ref[:, after], high_t_ref[to, :], low_t_ref[to, :])


def second_kernel(factor, own_ref, oth_ref, im_own_ref, im_oth_ref, near_ref, high_ref, low_ref, *refs):
    dir_ref, res_ref, image_ref, curve_ref, stat_ref, vec_ref, acc_ref = refs
    cols, half = im_own_ref.shape
    places = [slice(c, c + LANES) for c in range(0, half, LANES)]
    for at in places:
        vec_ref[0:cols, at], vec_ref[cols : 2 * cols, at] = split(im_oth_ref[:, at] * factor)
    acc_ref[...] = near_ref[...] + im_own_ref[...] / own_ref[cols + 3 : cols + 4, :]
    for r in range(0, half, 2 * PANEL):
        rows = slice(r, r + 2 * PANEL)
        acc_ref[...] += product(vec_ref[:, rows], high_ref[rows, :], low_ref[rows, :])
    blocks = [(ref, im, at) for ref, im in ((own_ref, im_own_ref), (oth_ref, im_oth_ref)) for at in places]
    zero = jnp.zeros((cols, LANES), F32)
    norm, curve, fresh = zero, zero, zero
    for ref, im, at in blocks:
        value = ref[0:cols, at]
        norm = norm + value * value
        curve = curve + value * im[:, at]
    norm = jnp.sum(norm, axis=1, keepdims=True)
    step = norm / jnp.sum(curve, axis=1, keepdims=True)
    for ref, im, at in blocks:
        value = ref[0:cols, at] - step * im[:, at]
        fresh = fresh + value * value
    fresh = jnp.sum(fresh, axis=1, keepdims=True)
    ratio = fresh / norm
    curve = zero
    for at in places:
        value, first = own_ref[0:cols, at], im_own_ref[:, at]
        left = value - step * first
        direction = left + ratio * value
        image = first + (ratio * first - step * acc_ref[:, at])
        res_ref[:, at] = left
        dir_ref[:, at] = direction
        image_ref[:, at] = image
        curve = curve + direction * image
    curve_ref[...] = curve
    stat_ref[0] = jnp.broadcast_to(step, (cols, LANES))
    stat_ref[1] = jnp.broadcast_to(fresh, (cols, LANES))


def last_kernel(own_ref, dir_ref, res_ref, image_ref, curve_ref, other_ref, stat_ref, out_ref):
    cols, half = own_ref.shape[0] - EXTRA, own_ref.shape[1]
    parts = half // LANES
    curve = jnp.sum(curve_ref[...] + other_ref[...], axis=1, keepdims=True)
    first = stat_ref[0, :, 0:1]
    step = stat_ref[1, :, 0:1] / curve
    for q in range(parts):
        at = slice(q * LANES, (q + 1) * LANES)
        out_ref[q, 0:cols, :] = first * own_ref[0:cols, at] + step * dir_ref[:, at]
        out_ref[q, cols : 2 * cols, :] = res_ref[:, at] - step * image_ref[:, at]


def unpack_kernel(in_ref, sol_hbm, res_hbm, sol_ref, res_ref, sems):
    parts, cols = in_ref.shape[0], in_ref.shape[1] // 2
    copies = []
    for n, (ref, out) in enumerate(((sol_ref, sol_hbm), (res_ref, res_hbm))):
        ref[...] = in_ref[:, n * cols : (n + 1) * cols, :].reshape(parts * cols, LANES).T
        copies.append(pltpu.make_async_copy(ref, out, sems.at[n]))
        copies[-1].start()
    for copy in copies:
        copy.wait()


def shape(*dims, dtype=F32):
    return jax.ShapeDtypeStruct(dims, dtype)


def call(kernel, out, ins, scratch=(), limit=8, where=VM):
    return pl.pallas_call(
        kernel,
        out_shape=out,
        in_specs=ins,
        out_specs=[where] * len(out),
        scratch_shapes=list(scratch),
        compiler_params=pltpu.CompilerParams(vmem_limit_bytes=limit << 20),
    )


def by_columns(positions, radii, right_side):
    row_size, col_size = lax.axis_size("row"), lax.axis_size("col")
    devices = row_size * col_size
    parts = devices // 2
    rows, columns = right_side.shape
    total = rows * devices
    cols = columns // parts
    half = total // 2
    panels = half // PANEL
    kernel_scale, softening = constants(total)
    soft, factor = softening * 4.0**9, kernel_scale * 2.0**9
    groups = [[2 * chip + core for chip in range(parts)] for core in range(2)]
    swap = [(i, i ^ 1) for i in range(col_size)]

    (packed,) = call(
        functools.partial(pack_kernel, parts),
        [shape(parts, cols // EXTRA + 1, EXTRA, LANES)],
        [pl.BlockSpec(memory_space=pltpu.HBM)] * 3,
        [
            pltpu.VMEM((3, LANES), F32),
            pltpu.VMEM((1, LANES), F32),
            pltpu.VMEM((LANES, columns), F32),
            pltpu.SemaphoreType.DMA((COPIES + 2,)),
        ],
    )(*[pltpu.with_memory_space_constraint(x, pltpu.HBM) for x in (positions, radii.reshape(1, -1), right_side)])
    own = lax.all_to_all(packed, AXES, 0, 0, axis_index_groups=groups, tiled=True)
    oth = lax.ppermute(own, "col", swap)
    size = sum(cs.stop - cs.start for _, cs, _ in near_spans(panels))
    *near, right, acc, own_flat = call(
        functools.partial(first_kernel, soft, factor),
        [shape(PANEL, size, dtype=BF16)] * 2
        + [shape(size - half, PANEL, dtype=BF16)] * 2
        + [shape(DEPTH, half, dtype=BF16), shape(cols, half), shape(cols + EXTRA, half)],
        [VM],
        [
            pltpu.VMEM((2 * cols, half), BF16),
            pltpu.VMEM((half, DEPTH), BF16),
            pltpu.VMEM((DEPTH, half), F32),
        ],
        16,
    )(own)
    *across, image, oth_flat = call(
        functools.partial(middle_kernel, soft, factor),
        [shape(half, half, dtype=BF16)] * 2 + [shape(cols, half), shape(cols + EXTRA, half)],
        [VM] * 4,
        [
            pltpu.VMEM((2 * cols, half), BF16),
            pltpu.VMEM((half, DEPTH), BF16),
            pltpu.VMEM((DEPTH, half), F32),
        ],
        10,
    )(own_flat, oth, right, acc)
    image_oth = lax.ppermute(image, "col", swap)
    vec = pltpu.VMEM((2 * cols, half), BF16)
    (begun,) = call(functools.partial(near_kernel, factor), [shape(cols, half)], [VM] * 5, [vec])(image, *near)
    direction, residual, second, curve, stats = call(
        functools.partial(second_kernel, factor),
        [shape(cols, half)] * 3 + [shape(cols, LANES), shape(2, cols, LANES)],
        [VM] * 7,
        [vec, pltpu.VMEM((cols, half), F32)],
    )(own_flat, oth_flat, image, image_oth, begun, *across)
    (mixed,) = call(last_kernel, [shape(parts, 2 * cols, LANES)], [VM] * 7)(
        own_flat, direction, residual, second, curve, lax.ppermute(curve, "col", swap), stats
    )
    mixed = lax.all_to_all(mixed, AXES, 0, 0, axis_index_groups=groups, tiled=True)
    turned = [pltpu.VMEM((LANES, columns), F32)] * 2 + [pltpu.SemaphoreType.DMA((2,))]
    return tuple(call(unpack_kernel, [shape(LANES, columns)] * 2, [VM], turned, where=pl.BlockSpec(memory_space=pltpu.HBM))(mixed))


def body(positions, radii, right_side):
    devices = lax.axis_size("row") * lax.axis_size("col")
    rows, columns = right_side.shape
    total = rows * devices
    fits = rows == LANES and total % (4 * PANEL) == 0 and 16 * devices == 2 * columns
    if fits and 2 * total * total <= KERNEL_BYTES:
        return by_columns(positions, radii, right_side)
    return blockwise(positions, radii, right_side)


def solution(mesh):
    return jax.shard_map(
        body,
        mesh=mesh,
        in_specs=(P(None, ("row", "col")), P(("row", "col")), P(("row", "col"), None)),
        out_specs=(P(("row", "col"), None), P(("row", "col"), None)),
        check_vma=False,
    )
```
